128 devices in a mesh: expert: 16 (over z_lo, x, core), etp: 8 (over y, z_hi).
Axes of the slice: x: 4, y: 4, z: 4 (z_hi: 2, z_lo: 2; z = z_hi * 2 + z_lo), core: 2. Of those that a mesh axis runs over, the one named last changes fastest.
Arguments:
- tokens: bfloat16 [16384, 4096], P(('expert', 'etp')), may hold values from -6 to 6
- grad_out: bfloat16 [16384, 4096], P(('expert', 'etp')), may hold values from -6 to 6
- route_prob: float32 [16384], P(('expert', 'etp')), may hold values from 0.1 to 1
- expert_index: int32 [16384, 1], P(('expert', 'etp')), may hold values from 0 to 15; in each aligned block of 128 rows (0 to 127, 128 to 255, ...) at most 16 rows name the same one
- w_gate: bfloat16 [16, 4096, 4096], P('expert', None, 'etp'), may hold values from -0.09375 to 0.09375
- w_up: bfloat16 [16, 4096, 4096], P('expert', None, 'etp'), may hold values from -0.09375 to 0.09375
- w_down: bfloat16 [16, 4096, 4096], P('expert', 'etp'), may hold values from -0.09375 to 0.09375
Outputs:
- grad_tokens: bfloat16 [16384, 4096], P(('expert', 'etp'))
The draws below stay inside these ranges and needn't reach their ends.
Inputs may be any that keep to these rules, and one draw needn't show every extreme that they name: `expert_index`: in the 128 rows of one device no expert is named more than 16 times, a bound that some block reaches.
All inputs are finite; a program needn't handle non-finite values.
Results may differ from the reference program's by a relative error of at most 0.015.
Values may be sent and summed in bfloat16 or wider, within the bound.
A program may use at most 192 MiB of HBM per device.

```python
import math
import jax
import jax.numpy as jnp
import numpy as np
from jax import lax

D = 4096
FF = 4096
TOK_DEV = 128
EXPERTS = 16
CAP = 16
TOKENS = 16384
N_ETP = 8
DEVICES = 128


def levels(rng, shape, cuts, low, largest):
    factor_of, own = 1.0, jax.random.fold_in(rng, 6)
    for position, shards_of in cuts:
        steps = jnp.exp(jax.random.uniform(jax.random.fold_in(own, position), (shards_of,), jnp.float32, low / len(cuts), largest / len(cuts)))
        factor_of = factor_of * jnp.repeat(steps, shape[position] // shards_of).reshape([-1 if axis == position else 1 for axis in range(len(shape))])
    return factor_of


def assign_block(own_key, own, number, rows, count, top, most, lean):
    order = jax.random.permutation(own_key, count)
    packed, common = load_shares(count, rows * top, most, lean, True), load_shares(count, rows * top, most, lean, False)
    places = jnp.arange(count)

    def named(sizes, offset_by):
        used = int((sizes > 0).sum())
        fixed = max(1, used // 4)
        shifted = fixed + (places - fixed + offset_by * (used - fixed)) % max(1, count - fixed)
        return jnp.zeros((count,), jnp.int32).at[order[jnp.where(places < fixed, places, shifted)]].set(jnp.asarray(sizes, jnp.int32))

    sizes = jnp.where(number % 4 == 0, named(packed, number // 4), named(common, number - number // 4 - 1))
    mixed = jax.random.permutation(jax.random.fold_in(own, 3), count)
    donor, taker = mixed[0:count // 2 * 2:2], mixed[1:count // 2 * 2:2]
    slack = jnp.minimum(sizes[donor] - 1, most - sizes[taker]) // 2
    slack = jnp.where((donor == order[0]) | (taker == order[0]) | (sizes[taker] == 0), 0, jnp.maximum(slack, 0))
    shifted = jax.random.randint(jax.random.fold_in(own, 4), (count // 2,), 0, 1 << 20) % (slack + 1)
    sizes = sizes.at[donor].add(-shifted).at[taker].add(shifted)
    items = jnp.searchsorted(jnp.cumsum(sizes), jnp.arange(rows * top), side="right").astype(jnp.int32)
    grid = items.reshape(top, rows).T
    grid = grid[jax.random.permutation(jax.random.fold_in(own, 1), rows)]
    offset_by = jax.random.randint(jax.random.fold_in(own, 2), (rows, 1), 0, top)
    return jnp.take_along_axis(grid, (jnp.arange(top)[None, :] + offset_by) % top, axis=1)


def load_shares(count, total, most, skew, full):
    portions = [(1 << 20) // math.isqrt(standing ** skew) + 1 for standing in range(1, count + 1)]
    largest = most if full else min(most, max(-(-total // count), total * portions[0] // sum(portions)))
    least = 1 if total - largest >= count - 1 else 0
    holding, rest = [largest] + [least] * (count - 1), total - largest - least * (count - 1)
    while rest > 0:
        movable = [i for i in range(1, count) if holding[i] < largest] or [i for i in range(1, count) if holding[i] < most]
        whole, budget = sum([portions[i] for i in movable]), rest
        for i in movable:
            more = min(most - holding[i], max(1, budget * portions[i] // whole), rest)
            holding[i] = holding[i] + more
            rest = rest - more
    return np.array(holding)


def gaussian(rng, shape, width, limit, shards=(), held_as=jnp.bfloat16):
    drawn = width * jax.random.normal(rng, shape, jnp.float32)
    if shards:
        drawn = drawn * levels(rng, shape, shards, -0.22, 0.18)
    return jnp.clip(drawn, -limit, limit).astype(held_as)


def setup_inputs(seed: int = 0) -> dict:
    key_of = jax.random.split(jax.random.key(seed), 8)
    tokens = gaussian(key_of[0], (TOKENS, D), 1.0, 6.0, ((0, 128),))
    grad_out = gaussian(key_of[1], (TOKENS, D), 1.0, 6.0, ((0, 128),))
    route_prob = jnp.clip(jnp.exp(math.log(1.0) - 2.3025851 * jax.random.uniform(key_of[2], (TOKENS,), jnp.float32) ** levels(key_of[2], (TOKENS,), ((0, 128),), -0.2, 0.2)), 0.1, 1.0)
    expert_index_keys = jax.random.split(jax.random.fold_in(key_of[3], 1), TOKENS // TOK_DEV)
    expert_index_turns = jax.random.permutation(jax.random.fold_in(key_of[3], 3), TOKENS // TOK_DEV)
    expert_index = jax.vmap(lambda own, number: assign_block(jax.random.fold_in(key_of[3], 2), own, number, TOK_DEV, EXPERTS, 1, CAP, 2))(expert_index_keys, expert_index_turns).reshape((TOKENS, 1))
    w_gate = gaussian(key_of[4], (EXPERTS, D, FF), D ** -0.5, 0.09375, ((0, 16), (2, 8)))
    w_up = gaussian(key_of[5], (EXPERTS, D, FF), D ** -0.5, 0.09375, ((0, 16), (2, 8)))
    w_down = gaussian(key_of[6], (EXPERTS, FF, D), FF ** -0.5, 0.09375, ((0, 16), (1, 8)))
    return dict(tokens=tokens, grad_out=grad_out, route_prob=route_prob, expert_index=expert_index, w_gate=w_gate, w_up=w_up, w_down=w_down)


def expert_terms(rows_x, rows_grad, gate_local, up_local, down_local):
    gate_proj = jnp.dot(rows_x, gate_local, preferred_element_type=jnp.float32)
    up_proj = jnp.dot(rows_x, up_local, preferred_element_type=jnp.float32)
    hidden_grad = jnp.dot(rows_grad, down_local.T, preferred_element_type=jnp.float32)
    sigma = jax.nn.sigmoid(gate_proj)
    slope = sigma * (1.0 + gate_proj * (1.0 - sigma))
    gate_grad = (hidden_grad * up_proj * slope).astype(jnp.bfloat16)
    up_grad = (hidden_grad * gate_proj * sigma).astype(jnp.bfloat16)
    return jnp.dot(gate_grad, gate_local.T, preferred_element_type=jnp.float32) + jnp.dot(up_grad, up_local.T, preferred_element_type=jnp.float32)


def one_expert(operands):
    rows_x, rows_grad, gate_full, up_full, down_full = operands
    block = FF // N_ETP
    total = jnp.zeros((rows_x.shape[0], D), jnp.float32)
    for member in range(N_ETP):
        lower = member * block
        partial_term = expert_terms(rows_x, rows_grad, gate_full[:, lower:lower + block], up_full[:, lower:lower + block], down_full[lower:lower + block, :])
        rounded = lax.optimization_barrier(partial_term.astype(jnp.bfloat16))
        total = total + rounded.astype(jnp.float32)
    return total.astype(jnp.bfloat16)


def reference(tokens, grad_out, route_prob, expert_index, w_gate, w_up, w_down):
    expert_ids = expert_index[:, 0].reshape(DEVICES, TOK_DEV)
    chosen = (expert_ids[:, :, None] == jnp.arange(EXPERTS, dtype=jnp.int32)[None, None, :]).astype(jnp.int32)
    before = jnp.cumsum(chosen, axis=1) - chosen
    slot_index = jnp.sum(before * chosen, axis=2)
    source = jnp.arange(DEVICES, dtype=jnp.int32)[:, None]
    slot_place = (expert_ids * (DEVICES * CAP) + source * CAP + slot_index).reshape(-1).astype(jnp.int32)
    scaled = (route_prob[:, None] * grad_out.astype(jnp.float32)).astype(jnp.bfloat16)
    rows_x = jnp.zeros((EXPERTS * DEVICES * CAP, D), jnp.bfloat16).at[slot_place].set(tokens)
    rows_grad = jnp.zeros((EXPERTS * DEVICES * CAP, D), jnp.bfloat16).at[slot_place].set(scaled)
    rows_x = rows_x.reshape(EXPERTS, DEVICES * CAP, D)
    rows_grad = rows_grad.reshape(EXPERTS, DEVICES * CAP, D)
    results = lax.map(one_expert, (rows_x, rows_grad, w_gate, w_up, w_down))
    return results.reshape(-1, D)[slot_place]
```

```python
import functools

import jax
import jax.numpy as jnp
from jax import lax
from jax.experimental import pallas as pl
from jax.experimental.pallas import tpu as pltpu
from jax.sharding import PartitionSpec as P

MESH = pl.DeviceIdType.MESH
BF16 = jnp.bfloat16
F32 = jnp.float32
D = 4096
UNITS = 512
CHUNKS = 4
SLOTS = 16
BLOCK = 4 * SLOTS
HALF = 4 * BLOCK
ROWS = 2 * HALF
EXPERTS = 16
COLS = 512
NT = (((1,), (1,)), ((), ()))


def mod4(value):
    return lax.rem(value + 8, 4)


def place(x, y, z, core):
    return (lax.rem(z, 2) * 4 + x) * 2 + core, y * 2 + z // 2


def kernel(
    tok, grad, prob, slot, w_gate, w_up, w_down,
    ret,
    rows, gate_v, up_v, down_v, send, land,
    a2a_s, a2a_r, ag_s, ag_r, fw_s, fw_r, sh_s, sh_r, w_s, w_r,
    sib_s, sib_r, half_s, half_r, full_s, full_r, ret_s, ret_r,
    cr_sib, cr_left, cr_right,
):
    e = lax.axis_index("expert")
    t = lax.axis_index("etp")
    core = lax.rem(e, 2)
    x = lax.rem(e // 2, 4)
    y = t // 2
    z_hi = lax.rem(t, 2)
    z = z_hi * 2 + e // 8
    other = 1 - core
    mine = (lax.rem(z, 2) * 4 + x) * 2 + z_hi
    y_right, y_left, y_far = mod4(y + 1), mod4(y - 1), mod4(y + 2)
    right, left = place(x, y_right, z, core), place(x, y_left, z, core)
    sibling = place(x, y, z, other)
    partner = place(x, y, mod4(z + 2), other)
    away = core != z_hi

    barrier = pltpu.get_barrier_semaphore()

    def greet(who):
        pl.semaphore_signal(barrier, inc=1, device_id=who, device_id_type=MESH)

    for k in range(1, 16):
        greet(place(mod4(x + k // 4), y, mod4(z + k % 4), core))
    for who in (right, left, sibling, partner):
        greet(who)

    onehot = (
        lax.broadcasted_iota(jnp.int32, (EXPERTS * SLOTS, tok.shape[0]), 0) == slot[...]
    ).astype(BF16)

    def fill(n, carry):
        cs = pl.ds(pl.multiple_of(n * COLS, COLS), COLS)
        send[0, :, cs] = jnp.dot(onehot, tok[:, cs], preferred_element_type=F32).astype(BF16)
        scaled = (prob[...] * grad[:, cs].astype(F32)).astype(BF16)
        send[1, :, cs] = jnp.dot(onehot, scaled, preferred_element_type=F32).astype(BF16)
        return carry

    lax.fori_loop(0, D // COLS, fill, 0)
    pl.semaphore_wait(barrier, 19)

    def remote(src, dst, s, r, who):
        return pltpu.make_async_remote_copy(
            src_ref=src, dst_ref=dst, send_sem=s, recv_sem=r, device_id=who, device_id_type=MESH
        )

    def rds(half, yo, off=0, n=BLOCK):
        return pl.ds(pl.multiple_of(half * HALF + yo * BLOCK + off, SLOTS), n)

    def a2a(j, dz):
        xd, zd = mod4(x + j + dz), mod4(z + dz)
        ed = (lax.rem(zd, 2) * 4 + xd) * 2 + zd // 2
        src = send.at[:, pl.ds(pl.multiple_of(ed * SLOTS, SLOTS), SLOTS), :]
        dst = rows.at[j, :, rds(core, y, dz * SLOTS, SLOTS), :]
        if j == 0 and dz == 0:
            return pltpu.make_async_copy(src, dst, a2a_r.at[0])
        return remote(src, dst, a2a_s.at[j * 4 + dz], a2a_r.at[j * 4 + dz], place(xd, y, zd, core))

    for j in range(CHUNKS):
        for dz in range(4):
            a2a(j, dz).start()

    def own(j, direction):
        ref = rows.at[j, :, rds(core, y), :]
        return remote(ref, ref, ag_s.at[j, direction], ag_r.at[j, direction], (right, left)[direction])

    def own_in(j, direction):
        ref = rows.at[j, :, rds(core, (y_left, y_right)[direction]), :]
        return remote(ref, ref, ag_s.at[j, direction], ag_r.at[j, direction], (right, left)[direction])

    def forward(j, direction):
        ref = rows.at[j, direction, rds(core, (y_left, y_right)[direction]), :]
        return remote(ref, ref, fw_s.at[j, direction], fw_r.at[j, direction], (right, left)[direction])

    def forward_in(j, direction):
        ref = rows.at[j, direction, rds(core, y_far), :]
        return remote(ref, ref, fw_s.at[j, direction], fw_r.at[j, direction], (right, left)[direction])

    def share(j, k, half):
        ref = rows.at[j, :, rds(half, mod4(y + k)), :]
        return remote(ref, ref, sh_s.at[j, k], sh_r.at[j, k], sibling)

    weights = ((w_gate, gate_v), (w_up, up_v), (w_down, down_v))

    def weight_in(k):
        return pltpu.make_async_copy(weights[k][0], weights[k][1], w_r.at[k])

    def weight_out(k):
        return remote(weights[k][0], weights[k][1], w_s.at[k], w_r.at[k], partner)

    def start_weights():
        @pl.when(away)
        def _():
            for k in range(3):
                weight_out(k).start()

        @pl.when(jnp.logical_not(away))
        def _():
            for k in range(3):
                weight_in(k).start()

    for j in range(CHUNKS):
        for dz in range(4):
            if j == 0 and dz == 0:
                a2a(j, dz).wait()
            else:
                a2a(j, dz).wait_recv()
        own(j, 0).start()
        own(j, 1).start()
        share(j, 0, core).start()
        if j == 1:
            start_weights()

    for j in range(CHUNKS):
        own_in(j, 0).wait_recv()
        forward(j, 0).start()
        share(j, 3, core).start()
        own_in(j, 1).wait_recv()
        forward(j, 1).start()
        share(j, 1, core).start()
        if j == 0:
            for k in range(1, 16):
                a2a(k // 4, k % 4).wait_send()
            pl.semaphore_signal(cr_sib, inc=2, device_id=sibling, device_id_type=MESH)

    for j in range(CHUNKS):
        forward_in(j, 0).wait_recv()
        forward_in(j, 1).wait_recv()
        share(j, 2, core).start()

    for j in range(CHUNKS):
        for direction in range(2):
            own(j, direction).wait_send()
            forward(j, direction).wait_send()
        for k in range(4):
            share(j, k, core).wait_send()
            share(j, k, other).wait_recv()

    @pl.when(away)
    def _():
        for k in range(3):
            weight_out(k).wait()

    @pl.when(jnp.logical_not(away))
    def _():
        for k in range(3):
            weight_in(k).wait()

    def compute(j, half):
        rs = pl.ds(pl.multiple_of(half * HALF, HALF), HALF)
        xr = rows[j, 0, rs, :]
        gate = jnp.dot(xr, gate_v[...], preferred_element_type=F32)
        up = jnp.dot(xr, up_v[...], preferred_element_type=F32)
        hidden = lax.dot_general(rows[j, 1, rs, :], down_v[...], NT, preferred_element_type=F32)
        sigma = jax.nn.sigmoid(gate)
        slope = sigma * (1.0 + gate * (1.0 - sigma))
        gate_grad = (hidden * up * slope).astype(BF16)
        up_grad = (hidden * gate * sigma).astype(BF16)

        def columns(n, carry):
            cs = pl.ds(pl.multiple_of(n * COLS, COLS), COLS)
            part = lax.dot_general(gate_grad, gate_v[cs, :], NT, preferred_element_type=F32)
            part += lax.dot_general(up_grad, up_v[cs, :], NT, preferred_element_type=F32)
            rows[j, 0, rs, cs] = part.astype(BF16)
            return carry

        lax.fori_loop(0, D // COLS, columns, 0)

    def add(j, at, n, sources):
        def body(k, carry):
            cs = pl.ds(pl.multiple_of(k * COLS, COLS), COLS)
            total = rows[j, 0, at, cs].astype(F32)
            for ref, first in sources:
                total += ref[pl.ds(first, n), cs].astype(F32)
            rows[j, 0, at, cs] = total.astype(BF16)
            return carry

        lax.fori_loop(0, D // COLS, body, 0)

    def sib(j, half):
        src = rows.at[j, 0, pl.ds(pl.multiple_of(half * HALF, HALF), HALF), :]
        return remote(src, send.at[lax.rem(j, 2)], sib_s.at[j], sib_r.at[j], sibling)

    def half_sum(j, direction):
        first = direction * (BLOCK // 2)
        src = rows.at[j, 0, rds(core, y_far, first, BLOCK // 2), :]
        dst = land.at[lax.rem(j, 2), pl.ds(first, BLOCK // 2), :]
        return remote(src, dst, half_s.at[j, direction], half_r.at[j, direction], (right, left)[direction])

    def full_sum(j, direction):
        src = rows.at[j, 0, rds(core, (y_right, y_left)[direction]), :]
        dst = land.at[lax.rem(j, 2), pl.ds(BLOCK * (1 + direction), BLOCK), :]
        return remote(src, dst, full_s.at[j, direction], full_r.at[j, direction], (right, left)[direction])

    def back(j, dz, run):
        xs, zs = mod4(x - j - dz), mod4(z - dz)
        src = rows.at[j, 0, rds(core, y, dz * SLOTS, SLOTS), :]
        dst = ret.at[pl.ds(pl.multiple_of(mine * SLOTS, SLOTS), SLOTS), :]
        copy = remote(src, dst, ret_s.at[j * 4 + dz], ret_r.at[j * 4 + dz], place(xs, y, zs, core))
        if dz:
            run(copy)
            return

        @pl.when(j > 0)
        def _():
            run(copy)

    def local_back():
        src = rows.at[0, 0, rds(core, y, 0, SLOTS), :]
        dst = ret.at[pl.ds(pl.multiple_of(mine * SLOTS, SLOTS), SLOTS), :]
        return pltpu.make_async_copy(src, dst, ret_r.at[0])

    def stage_sib(j):
        sib(j, other).wait_recv()
        add(j, pl.ds(pl.multiple_of(core * HALF, HALF), HALF), HALF, [(send.at[lax.rem(j, 2)], 0)])

        @pl.when(j < CHUNKS - 2)
        def _():
            pl.semaphore_signal(cr_sib, inc=1, device_id=sibling, device_id_type=MESH)

        @pl.when(j >= 2)
        def _():
            pl.semaphore_wait(cr_right, 1)
            pl.semaphore_wait(cr_left, 1)

        half_sum(j, 0).start()
        half_sum(j, 1).start()

    def stage_half(j):
        lands = land.at[lax.rem(j, 2)]
        half_sum(j, 0).wait_recv()
        add(j, rds(core, y_right, 0, BLOCK // 2), BLOCK // 2, [(lands, 0)])
        full_sum(j, 0).start()
        half_sum(j, 1).wait_recv()
        add(j, rds(core, y_left, BLOCK // 2, BLOCK // 2), BLOCK // 2, [(lands, BLOCK // 2)])
        full_sum(j, 1).start()

    def stage_full(j):
        lands = land.at[lax.rem(j, 2)]
        full_sum(j, 0).wait_recv()
        full_sum(j, 1).wait_recv()
        add(j, rds(core, y), BLOCK, [(lands, BLOCK), (lands, 2 * BLOCK)])

        @pl.when(j < CHUNKS - 2)
        def _():
            pl.semaphore_signal(cr_right, inc=1, device_id=left, device_id_type=MESH)
            pl.semaphore_signal(cr_left, inc=1, device_id=right, device_id_type=MESH)

        for dz in range(4):
            back(j, dz, lambda copy: copy.start())

        @pl.when(j == 0)
        def _():
            local_back().start()

    def step(j, carry):
        compute(j, other)
        pl.semaphore_wait(cr_sib, 1)
        sib(j, other).start()

        @pl.when(j >= 1)
        def _():
            stage_half(j - 1)

        @pl.when(j >= 2)
        def _():
            stage_full(j - 2)

        compute(j, core)
        stage_sib(j)
        return carry

    lax.fori_loop(0, CHUNKS, step, 0)
    stage_half(CHUNKS - 1)
    stage_full(CHUNKS - 2)
    stage_full(CHUNKS - 1)

    def finish(j, carry):
        sib(j, other).wait_send()
        for direction in range(2):
            half_sum(j, direction).wait_send()
            full_sum(j, direction).wait_send()
        for dz in range(4):
            back(j, dz, lambda copy: copy.wait())
        return carry

    lax.fori_loop(0, CHUNKS, finish, 0)
    local_back().wait()


def shards(tokens, grad_out, route_prob, expert_index, w_gate, w_up, w_down):
    expert_ids = expert_index[:, 0]
    chosen = (expert_ids[:, None] == jnp.arange(EXPERTS, dtype=jnp.int32)[None, :]).astype(jnp.int32)
    before = jnp.cumsum(chosen, axis=0) - chosen
    slot = expert_ids * SLOTS + jnp.sum(before * chosen, axis=1)
    vmem = pl.BlockSpec(memory_space=pltpu.VMEM)
    hbm = pl.BlockSpec(memory_space=pl.ANY)
    dma = pltpu.SemaphoreType.DMA
    regular = pltpu.SemaphoreType.REGULAR
    returned = pl.pallas_call(
        kernel,
        out_shape=jax.ShapeDtypeStruct((EXPERTS * SLOTS, D), BF16),
        in_specs=[vmem] * 4 + [hbm] * 3,
        out_specs=hbm,
        scratch_shapes=[
            pltpu.VMEM((CHUNKS, 2, ROWS, D), BF16),
            pltpu.VMEM((D, UNITS), BF16),
            pltpu.VMEM((D, UNITS), BF16),
            pltpu.VMEM((UNITS, D), BF16),
            pltpu.VMEM((2, HALF, D), BF16),
            pltpu.VMEM((2, 3 * BLOCK, D), BF16),
            dma((16,)), dma((16,)),
            dma((CHUNKS, 2)), dma((CHUNKS, 2)),
            dma((CHUNKS, 2)), dma((CHUNKS, 2)),
            dma((CHUNKS, 4)), dma((CHUNKS, 4)),
            dma((3,)), dma((3,)),
            dma((CHUNKS,)), dma((CHUNKS,)),
            dma((CHUNKS, 2)), dma((CHUNKS, 2)),
            dma((CHUNKS, 2)), dma((CHUNKS, 2)),
            dma((16,)), dma((16,)),
            regular, regular, regular,
        ],
        compiler_params=pltpu.CompilerParams(
            collective_id=1, has_side_effects=True, vmem_limit_bytes=63 * 1024 * 1024
        ),
        cost_estimate=pl.CostEstimate(
            flops=2 * CHUNKS * ROWS * D * UNITS * 5, bytes_accessed=64 << 20, transcendentals=0
        ),
    )(tokens, grad_out, route_prob[:, None], slot[None, :], w_gate[0], w_up[0], w_down[0])
    return returned[slot]


def solution(mesh):
    return jax.shard_map(
        shards,
        mesh=mesh,
        in_specs=(
            P(("expert", "etp"), None),
            P(("expert", "etp"), None),
            P(("expert", "etp")),
            P(("expert", "etp"), None),
            P("expert", None, "etp"),
            P("expert", None, "etp"),
            P("expert", "etp", None),
        ),
        out_specs=P(("expert", "etp"), None),
        check_vma=False,
    )
```

```python
import functools

import jax
import jax.numpy as jnp
from jax import lax
from jax.experimental import pallas as pl
from jax.experimental.pallas import tpu as pltpu
from jax.sharding import PartitionSpec as P

MESH = pl.DeviceIdType.MESH
BF16 = jnp.bfloat16
F32 = jnp.float32
D = 4096
UNITS = 512
CHUNKS = 4
SLOTS = 16
BLOCK = 4 * SLOTS
HALF = 4 * BLOCK
ROWS = 2 * HALF
EXPERTS = 16
COLS = 512
PART = UNITS // 2
WIDE = D // 2
NT = (((1,), (1,)), ((), ()))


def mod4(value):
    return lax.rem(value + 8, 4)


def place(x, y, z, core):
    return (lax.rem(z, 2) * 4 + x) * 2 + core, y * 2 + z // 2


def kernel(
    tok, grad, prob, index, w_gate, w_up, w_down,
    out,
    rows, gate_v, up_v, down_v, send, land, ret, gate_t, up_t, onehot_t,
    a2a_s, a2a_r, ag_s, ag_r, fw_s, fw_r, sh_s, sh_r, w_s, w_r,
    sib_s, sib_r, half_s, half_r, full_s, full_r, ret_s, ret_r,
    cr_sib, cr_left, cr_right,
):
    e = lax.axis_index("expert")
    t = lax.axis_index("etp")
    core = lax.rem(e, 2)
    x = lax.rem(e // 2, 4)
    y = t // 2
    z_hi = lax.rem(t, 2)
    z = z_hi * 2 + e // 8
    other = 1 - core
    mine = (lax.rem(z, 2) * 4 + x) * 2 + z_hi
    y_right, y_left, y_far = mod4(y + 1), mod4(y - 1), mod4(y + 2)
    right, left = place(x, y_right, z, core), place(x, y_left, z, core)
    sibling = place(x, y, z, other)
    partner = place(x, y, mod4(z + 2), other)
    away = core != z_hi

    barrier = pltpu.get_barrier_semaphore()

    def greet(who):
        pl.semaphore_signal(barrier, inc=1, device_id=who, device_id_type=MESH)

    for k in range(1, 16):
        greet(place(mod4(x + k // 4), y, mod4(z + k % 4), core))
    for who in (right, left, sibling, partner):
        greet(who)

    n_tok = tok.shape[0]
    at_row = lax.broadcasted_iota(jnp.int32, (n_tok, n_tok), 0)
    at_col = lax.broadcasted_iota(jnp.int32, (n_tok, n_tok), 1)
    earlier = (at_row < at_col).astype(BF16)
    same = (at_row == at_col).astype(F32)
    ids = index[...]
    chosen = (lax.broadcasted_iota(jnp.int32, (EXPERTS, n_tok), 0) == ids).astype(F32)
    before = jnp.dot(chosen.astype(BF16), earlier, preferred_element_type=F32)
    slot = ids.astype(F32) * SLOTS + jnp.sum(before * chosen, axis=0, keepdims=True)
    slot_col = jnp.sum(same * slot, axis=1, keepdims=True)
    scale = jnp.sum(same * prob[...], axis=1, keepdims=True)
    n_slot = EXPERTS * SLOTS
    onehot = (lax.broadcasted_iota(jnp.int32, (n_slot, n_tok), 0).astype(F32) == slot).astype(BF16)
    onehot_t[...] = (
        lax.broadcasted_iota(jnp.int32, (n_tok, n_slot), 1).astype(F32) == slot_col
    ).astype(BF16)

    def fill(n, carry):
        cs = pl.ds(pl.multiple_of(n * COLS, COLS), COLS)
        send[0, :, cs] = jnp.dot(onehot, tok[:, cs], preferred_element_type=F32).astype(BF16)
        scaled = (scale * grad[:, cs].astype(F32)).astype(BF16)
        send[1, :, cs] = jnp.dot(onehot, scaled, preferred_element_type=F32).astype(BF16)
        return carry

    lax.fori_loop(0, D // COLS, fill, 0)
    pl.semaphore_wait(barrier, 19)

    def remote(src, dst, s, r, who):
        return pltpu.make_async_remote_copy(
            src_ref=src, dst_ref=dst, send_sem=s, recv_sem=r, device_id=who, device_id_type=MESH
        )

    def rds(half, yo, off=0, n=BLOCK):
        return pl.ds(pl.multiple_of(half * HALF + yo * BLOCK + off, SLOTS), n)

    def a2a(j, dz):
        xd, zd = mod4(x + j + dz), mod4(z + dz)
        ed = (lax.rem(zd, 2) * 4 + xd) * 2 + zd // 2
        src = send.at[:, pl.ds(pl.multiple_of(ed * SLOTS, SLOTS), SLOTS), :]
        dst = rows.at[j, :, rds(core, y, dz * SLOTS, SLOTS), :]
        if j == 0 and dz == 0:
            return pltpu.make_async_copy(src, dst, a2a_r.at[0])
        return remote(src, dst, a2a_s.at[j * 4 + dz], a2a_r.at[j * 4 + dz], place(xd, y, zd, core))

    for j in range(CHUNKS):
        for dz in range(4):
            a2a(j, dz).start()

    def own(j, direction):
        ref = rows.at[j, :, rds(core, y), :]
        return remote(ref, ref, ag_s.at[j, direction], ag_r.at[j, direction], (right, left)[direction])

    def own_in(j, direction):
        ref = rows.at[j, :, rds(core, (y_left, y_right)[direction]), :]
        return remote(ref, ref, ag_s.at[j, direction], ag_r.at[j, direction], (right, left)[direction])

    def forward(j, direction):
        ref = rows.at[j, direction, rds(core, (y_left, y_right)[direction]), :]
        return remote(ref, ref, fw_s.at[j, direction], fw_r.at[j, direction], (right, left)[direction])

    def forward_in(j, direction):
        ref = rows.at[j, direction, rds(core, y_far), :]
        return remote(ref, ref, fw_s.at[j, direction], fw_r.at[j, direction], (right, left)[direction])

    def share(j, k, half):
        ref = rows.at[j, :, rds(half, mod4(y + k)), :]
        return remote(ref, ref, sh_s.at[j, k], sh_r.at[j, k], sibling)

    def weight_refs(p, k):
        units = pl.ds(p * PART, PART)
        return (
            (w_gate.at[:, units], gate_v.at[p]),
            (w_up.at[:, units], up_v.at[p]),
            (w_down.at[units, :], down_v.at[p]),
        )[k]

    def weight_in(p, k):
        src, dst = weight_refs(p, k)
        return pltpu.make_async_copy(src, dst, w_r.at[p, k])

    def weight_out(p, k):
        src, dst = weight_refs(p, k)
        return remote(src, dst, w_s.at[p, k], w_r.at[p, k], partner)

    def start_weights(p):
        @pl.when(away)
        def _():
            for k in range(3):
                weight_out(p, k).start()

        @pl.when(jnp.logical_not(away))
        def _():
            for k in range(3):
                weight_in(p, k).start()

    def wait_weights(p):
        @pl.when(away)
        def _():
            for k in range(3):
                weight_out(p, k).wait()

        @pl.when(jnp.logical_not(away))
        def _():
            for k in range(3):
                weight_in(p, k).wait()

    for j in range(CHUNKS):
        for dz in range(4):
            if j == 0 and dz == 0:
                a2a(j, dz).wait()
            else:
                a2a(j, dz).wait_recv()
        own(j, 0).start()
        own(j, 1).start()
        share(j, 0, core).start()
        if j == 1:
            start_weights(0)

    for j in range(CHUNKS):
        own_in(j, 0).wait_recv()
        forward(j, 0).start()
        share(j, 3, core).start()
        own_in(j, 1).wait_recv()
        forward(j, 1).start()
        share(j, 1, core).start()
        if j == 1:
            start_weights(1)
        if j == 0:
            for k in range(1, 16):
                a2a(k // 4, k % 4).wait_send()
            pl.semaphore_signal(cr_sib, inc=2, device_id=sibling, device_id_type=MESH)

    for j in range(CHUNKS):
        forward_in(j, 0).wait_recv()
        forward_in(j, 1).wait_recv()
        share(j, 2, core).start()

    for j in range(CHUNKS):
        for direction in range(2):
            own(j, direction).wait_send()
            forward(j, direction).wait_send()
        for k in range(4):
            share(j, k, core).wait_send()
            share(j, k, other).wait_recv()

    def half_rows(half):
        return pl.ds(pl.multiple_of(half * HALF, HALF), HALF)

    def terms(j, half, p):
        rs = half_rows(half)
        xr = rows[j, 0, rs, :]
        gate = jnp.dot(xr, gate_v[p], preferred_element_type=F32)
        up = jnp.dot(xr, up_v[p], preferred_element_type=F32)
        hidden = lax.dot_general(rows[j, 1, rs, :], down_v[p], NT, preferred_element_type=F32)
        sigma = jax.nn.sigmoid(gate)
        slope = sigma * (1.0 + gate * (1.0 - sigma))
        return (hidden * up * slope).astype(BF16), (hidden * gate * sigma).astype(BF16)

    def products(j, half, last, ch, received):
        rs = half_rows(half)
        gate_last, up_last = last

        def columns(n, carry):
            cs = pl.ds(pl.multiple_of(ch * WIDE + n * COLS, COLS), COLS)
            part = lax.dot_general(gate_t[j, rs, :], gate_v[0, cs, :], NT, preferred_element_type=F32)
            part += lax.dot_general(up_t[j, rs, :], up_v[0, cs, :], NT, preferred_element_type=F32)
            part += lax.dot_general(gate_last, gate_v[1, cs, :], NT, preferred_element_type=F32)
            part += lax.dot_general(up_last, up_v[1, cs, :], NT, preferred_element_type=F32)
            if received:
                part += send[lax.rem(j, 2), :, cs].astype(F32)
            rows[j, 0, rs, cs] = part.astype(BF16)
            return carry

        lax.fori_loop(0, WIDE // COLS, columns, 0)

    def add(j, at, n, ch, sources):
        def body(k, carry):
            cs = pl.ds(pl.multiple_of(ch * WIDE + k * COLS, COLS), COLS)
            total = rows[j, 0, at, cs].astype(F32)
            for first in sources:
                total += land[lax.rem(j, 2), pl.ds(first, n), cs].astype(F32)
            rows[j, 0, at, cs] = total.astype(BF16)
            return carry

        lax.fori_loop(0, WIDE // COLS, body, 0)

    def wide(ch):
        return pl.ds(ch * WIDE, WIDE)

    def sib(j, ch):
        src = rows.at[j, 0, half_rows(other), wide(ch)]
        dst = send.at[lax.rem(j, 2), :, wide(ch)]
        return remote(src, dst, sib_s.at[j, ch], sib_r.at[j, ch], sibling)

    def half_sum(j, ch, direction):
        first = direction * (BLOCK // 2)
        src = rows.at[j, 0, rds(core, y_far, first, BLOCK // 2), wide(ch)]
        dst = land.at[lax.rem(j, 2), pl.ds(first, BLOCK // 2), wide(ch)]
        k = 2 * ch + direction
        return remote(src, dst, half_s.at[j, k], half_r.at[j, k], (right, left)[direction])

    def full_sum(j, ch, direction):
        src = rows.at[j, 0, rds(core, (y_right, y_left)[direction]), wide(ch)]
        dst = land.at[lax.rem(j, 2), pl.ds(BLOCK * (1 + direction), BLOCK), wide(ch)]
        k = 2 * ch + direction
        return remote(src, dst, full_s.at[j, k], full_r.at[j, k], (right, left)[direction])

    def back_refs(j, ch, dz):
        src = rows.at[j, 0, rds(core, y, dz * SLOTS, SLOTS), wide(ch)]
        dst = ret.at[pl.ds(pl.multiple_of(mine * SLOTS, SLOTS), SLOTS), wide(ch)]
        return src, dst

    def back(j, ch, dz):
        src, dst = back_refs(j, ch, dz)
        who = place(mod4(x - j - dz), y, mod4(z - dz), core)
        return remote(src, dst, ret_s.at[j * 4 + dz, ch], ret_r.at[j * 4 + dz, ch], who)

    def local_back(ch):
        src, dst = back_refs(0, ch, 0)
        return pltpu.make_async_copy(src, dst, ret_r.at[0, ch])

    def stage_half(j, ch):
        half_sum(j, ch, 0).wait_recv()
        add(j, rds(core, y_right, 0, BLOCK // 2), BLOCK // 2, ch, [0])
        full_sum(j, ch, 0).start()
        half_sum(j, ch, 1).wait_recv()
        add(j, rds(core, y_left, BLOCK // 2, BLOCK // 2), BLOCK // 2, ch, [BLOCK // 2])
        full_sum(j, ch, 1).start()

    def stage_full(j, ch):
        full_sum(j, ch, 0).wait_recv()
        full_sum(j, ch, 1).wait_recv()
        add(j, rds(core, y), BLOCK, ch, [BLOCK, 2 * BLOCK])
        for dz in range(1, 4):
            back(j, ch, dz).start()

        @pl.when(j > 0)
        def _():
            back(j, ch, 0).start()

        @pl.when(j == 0)
        def _():
            local_back(ch).start()

    def credit(j):
        @pl.when(j < CHUNKS - 2)
        def _():
            pl.semaphore_signal(cr_right, inc=1, device_id=left, device_id_type=MESH)
            pl.semaphore_signal(cr_left, inc=1, device_id=right, device_id_type=MESH)

    wait_weights(0)

    def early(j, carry):
        for half in (other, core):
            gate_part, up_part = terms(j, half, 0)
            gate_t[j, half_rows(half), :] = gate_part
            up_t[j, half_rows(half), :] = up_part
        return carry

    lax.fori_loop(0, CHUNKS, early, 0)
    wait_weights(1)

    def step(j, carry):
        last = terms(j, other, 1)
        pl.semaphore_wait(cr_sib, 1)
        for ch in range(2):
            products(j, other, last, ch, False)
            sib(j, ch).start()

        @pl.when(j >= 1)
        def _():
            stage_half(j - 1, 1)

        last = terms(j, core, 1)

        @pl.when(j >= 1)
        def _():
            stage_full(j - 1, 0)

        @pl.when(j >= 2)
        def _():
            pl.semaphore_wait(cr_right, 1)
            pl.semaphore_wait(cr_left, 1)

        for ch in range(2):
            sib(j, ch).wait_recv()
            products(j, core, last, ch, True)
            half_sum(j, ch, 0).start()
            half_sum(j, ch, 1).start()

        @pl.when(j < CHUNKS - 2)
        def _():
            pl.semaphore_signal(cr_sib, inc=1, device_id=sibling, device_id_type=MESH)

        @pl.when(j >= 1)
        def _():
            stage_full(j - 1, 1)
            credit(j - 1)

        stage_half(j, 0)
        return carry

    lax.fori_loop(0, CHUNKS, step, 0)
    stage_half(CHUNKS - 1, 1)
    stage_full(CHUNKS - 1, 0)
    stage_full(CHUNKS - 1, 1)

    for ch in range(2):
        local_back(ch).wait()
        for k in range(1, 16):
            back(k // 4, ch, k % 4).wait_recv()

        def pick(n, carry):
            cs = pl.ds(pl.multiple_of(ch * WIDE + n * COLS, COLS), COLS)
            out[:, cs] = jnp.dot(onehot_t[...], ret[:, cs], preferred_element_type=F32).astype(BF16)
            return carry

        lax.fori_loop(0, WIDE // COLS, pick, 0)

    for ch in range(2):
        for k in range(1, 16):
            back(k // 4, ch, k % 4).wait_send()

    def finish(j, carry):
        for ch in range(2):
            sib(j, ch).wait_send()
            for direction in range(2):
                half_sum(j, ch, direction).wait_send()
                full_sum(j, ch, direction).wait_send()
        return carry

    lax.fori_loop(0, CHUNKS, finish, 0)


def shards(tokens, grad_out, route_prob, expert_index, w_gate, w_up, w_down):
    vmem = pl.BlockSpec(memory_space=pltpu.VMEM)
    hbm = pl.BlockSpec(memory_space=pl.ANY)
    dma = pltpu.SemaphoreType.DMA
    regular = pltpu.SemaphoreType.REGULAR
    n_tok = tokens.shape[0]
    return pl.pallas_call(
        kernel,
        out_shape=jax.ShapeDtypeStruct((n_tok, D), BF16),
        in_specs=[vmem] * 4 + [hbm] * 3,
        out_specs=vmem,
        scratch_shapes=[
            pltpu.VMEM((CHUNKS, 2, ROWS, D), BF16),
            pltpu.VMEM((2, D, PART), BF16),
            pltpu.VMEM((2, D, PART), BF16),
            pltpu.VMEM((2, PART, D), BF16),
            pltpu.VMEM((2, HALF, D), BF16),
            pltpu.VMEM((2, 3 * BLOCK, D), BF16),
            pltpu.VMEM((EXPERTS * SLOTS, D), BF16),
            pltpu.VMEM((CHUNKS, ROWS, PART), BF16),
            pltpu.VMEM((CHUNKS, ROWS, PART), BF16),
            pltpu.VMEM((n_tok, EXPERTS * SLOTS), BF16),
            dma((16,)), dma((16,)),
            dma((CHUNKS, 2)), dma((CHUNKS, 2)),
            dma((CHUNKS, 2)), dma((CHUNKS, 2)),
            dma((CHUNKS, 4)), dma((CHUNKS, 4)),
            dma((2, 3)), dma((2, 3)),
            dma((CHUNKS, 2)), dma((CHUNKS, 2)),
            dma((CHUNKS, 4)), dma((CHUNKS, 4)),
            dma((CHUNKS, 4)), dma((CHUNKS, 4)),
            dma((16, 2)), dma((16, 2)),
            regular, regular, regular,
        ],
        compiler_params=pltpu.CompilerParams(
            collective_id=1, has_side_effects=True, vmem_limit_bytes=63 * 1024 * 1024
        ),
        cost_estimate=pl.CostEstimate(
            flops=2 * CHUNKS * ROWS * D * UNITS * 5, bytes_accessed=64 << 20, transcendentals=0
        ),
    )(
        tokens, grad_out, route_prob.reshape(1, n_tok), expert_index.reshape(1, n_tok),
        w_gate[0], w_up[0], w_down[0],
    )


def solution(mesh):
    return jax.shard_map(
        shards,
        mesh=mesh,
        in_specs=(
            P(("expert", "etp"), None),
            P(("expert", "etp"), None),
            P(("expert", "etp")),
            P(("expert", "etp"), None),
            P("expert", None, "etp"),
            P("expert", None, "etp"),
            P("expert", "etp", None),
        ),
        out_specs=P(("expert", "etp"), None),
        check_vma=False,
    )
```

```python
import functools

import jax
import jax.numpy as jnp
from jax import lax
from jax.experimental import pallas as pl
from jax.experimental.pallas import tpu as pltpu
from jax.sharding import PartitionSpec as P

MESH = pl.DeviceIdType.MESH
BF16 = jnp.bfloat16
F32 = jnp.float32
D = 4096
UNITS = 512
CHUNKS = 4
SLOTS = 16
BLOCK = 4 * SLOTS
HALF = 4 * BLOCK
ROWS = 2 * HALF
EXPERTS = 16
COLS = 512
PIECES = ((0, 384), (384, 128))
WIDTHS = 4
WIDE = D // WIDTHS
STEPS = (
    ((0, 0), (1, 1), (2, 2), (3, 3)),
    ((1, 0), (2, 1), (3, 2), (0, 3)),
    ((2, 0), (3, 1), (0, 2), (1, 3)),
    ((3, 0), (0, 1), (1, 2), (2, 3)),
)
NT = (((1,), (1,)), ((), ()))


def mod4(value):
    return lax.rem(value + 8, 4)


def step_of(j, k):
    if isinstance(j, int):
        return STEPS[j][k]
    dx, dz = STEPS[0][k]
    for t in range(1, CHUNKS):
        dx = jnp.where(j == t, STEPS[t][k][0], dx)
        dz = jnp.where(j == t, STEPS[t][k][1], dz)
    return dx, dz


def place(x, y, z, core):
    return (lax.rem(z, 2) * 4 + x) * 2 + core, y * 2 + z // 2


def kernel(
    tok_h, grad_h, prob, index, w_gate, w_up, w_down,
    out,
    rows, gu_v, down_v, send, ret, terms_v, onehot_t, tok, grad, in_s,
    a2a_s, a2a_r, ag_s, ag_r, fw_s, fw_r, sh_s, sh_r, w_s, w_r,
    sib_s, sib_r, half_s, half_r, full_s, full_r, ret_s, ret_r,
    cr_sib, cr_left, cr_right,
):
    e = lax.axis_index("expert")
    t = lax.axis_index("etp")
    core = lax.rem(e, 2)
    x = lax.rem(e // 2, 4)
    y = t // 2
    z_hi = lax.rem(t, 2)
    z = z_hi * 2 + e // 8
    other = 1 - core
    mine = (lax.rem(z, 2) * 4 + x) * 2 + z_hi
    y_right, y_left, y_far = mod4(y + 1), mod4(y - 1), mod4(y + 2)
    right, left = place(x, y_right, z, core), place(x, y_left, z, core)
    sibling = place(x, y, z, other)
    partner = place(x, y, mod4(z + 2), other)
    away = core != z_hi

    tok_in = pltpu.make_async_copy(tok_h, tok, in_s.at[0])
    grad_in = pltpu.make_async_copy(grad_h, grad, in_s.at[1])
    tok_in.start()
    grad_in.start()

    barrier = pltpu.get_barrier_semaphore()

    def greet(who):
        pl.semaphore_signal(barrier, inc=1, device_id=who, device_id_type=MESH)

    for k in range(1, 16):
        greet(place(mod4(x + k // 4), y, mod4(z + k % 4), core))
    for who in (right, left, sibling, partner):
        greet(who)

    n_tok = tok.shape[0]
    at_row = lax.broadcasted_iota(jnp.int32, (n_tok, n_tok), 0)
    at_col = lax.broadcasted_iota(jnp.int32, (n_tok, n_tok), 1)
    earlier = (at_row < at_col).astype(BF16)
    same = (at_row == at_col).astype(F32)
    ids = index[...]
    chosen = (lax.broadcasted_iota(jnp.int32, (EXPERTS, n_tok), 0) == ids).astype(F32)
    before = jnp.dot(chosen.astype(BF16), earlier, preferred_element_type=F32)
    slot = ids.astype(F32) * SLOTS + jnp.sum(before * chosen, axis=0, keepdims=True)
    slot_col = jnp.sum(same * slot, axis=1, keepdims=True)
    scale = jnp.sum(same * prob[...], axis=1, keepdims=True)
    n_slot = EXPERTS * SLOTS
    onehot = (lax.broadcasted_iota(jnp.int32, (n_slot, n_tok), 0).astype(F32) == slot).astype(BF16)
    onehot_t[...] = (
        lax.broadcasted_iota(jnp.int32, (n_tok, n_slot), 1).astype(F32) == slot_col
    ).astype(BF16)

    def fill(n, carry):
        cs = pl.ds(pl.multiple_of(n * COLS, COLS), COLS)
        send[0, :, cs] = jnp.dot(onehot, tok[:, cs], preferred_element_type=F32).astype(BF16)
        scaled = (scale * grad[:, cs].astype(F32)).astype(BF16)
        send[1, :, cs] = jnp.dot(onehot, scaled, preferred_element_type=F32).astype(BF16)
        return carry

    tok_in.wait()
    grad_in.wait()
    lax.fori_loop(0, D // COLS, fill, 0)
    pl.semaphore_wait(barrier, 19)

    def remote(src, dst, s, r, who):
        return pltpu.make_async_remote_copy(
            src_ref=src, dst_ref=dst, send_sem=s, recv_sem=r, device_id=who, device_id_type=MESH
        )

    def rds(half, yo, off=0, n=BLOCK):
        return pl.ds(pl.multiple_of(half * HALF + yo * BLOCK + off, SLOTS), n)

    def a2a(j, k):
        dx, dz = step_of(j, k)
        xd, zd = mod4(x + dx), mod4(z + dz)
        ed = (lax.rem(zd, 2) * 4 + xd) * 2 + zd // 2
        src = send.at[:, pl.ds(pl.multiple_of(ed * SLOTS, SLOTS), SLOTS), :]
        dst = rows.at[j, :, rds(core, y, k * SLOTS, SLOTS), :]
        if j == 0 and k == 0:
            return pltpu.make_async_copy(src, dst, a2a_r.at[0])
        return remote(src, dst, a2a_s.at[j * 4 + k], a2a_r.at[j * 4 + k], place(xd, y, zd, core))

    for j in range(CHUNKS):
        for k in range(4):
            a2a(j, k).start()

    def own(j, direction):
        ref = rows.at[j, :, rds(core, y), :]
        return remote(ref, ref, ag_s.at[j, direction], ag_r.at[j, direction], (right, left)[direction])

    def own_in(j, direction):
        ref = rows.at[j, :, rds(core, (y_left, y_right)[direction]), :]
        return remote(ref, ref, ag_s.at[j, direction], ag_r.at[j, direction], (right, left)[direction])

    def forward(j, direction):
        ref = rows.at[j, direction, rds(core, (y_left, y_right)[direction]), :]
        return remote(ref, ref, fw_s.at[j, direction], fw_r.at[j, direction], (right, left)[direction])

    def forward_in(j, direction):
        ref = rows.at[j, direction, rds(core, y_far), :]
        return remote(ref, ref, fw_s.at[j, direction], fw_r.at[j, direction], (right, left)[direction])

    def share(j, k, half):
        ref = rows.at[j, :, rds(half, mod4(y + k)), :]
        return remote(ref, ref, sh_s.at[j, k], sh_r.at[j, k], sibling)

    def weight_refs(p, k):
        first, n = PIECES[p]
        units = pl.ds(first, n)
        return (
            (w_gate.at[:, units], gu_v.at[:, pl.ds(2 * first, n)]),
            (w_up.at[:, units], gu_v.at[:, pl.ds(2 * first + n, n)]),
            (w_down.at[units, :], down_v.at[units, :]),
        )[k]

    def weight_in(p, k):
        src, dst = weight_refs(p, k)
        return pltpu.make_async_copy(src, dst, w_r.at[p, k])

    def weight_out(p, k):
        src, dst = weight_refs(p, k)
        return remote(src, dst, w_s.at[p, k], w_r.at[p, k], partner)

    def start_weights(p):
        @pl.when(away)
        def _():
            for k in range(3):
                weight_out(p, k).start()

        @pl.when(jnp.logical_not(away))
        def _():
            for k in range(3):
                weight_in(p, k).start()

    def wait_weights(p):
        @pl.when(away)
        def _():
            for k in range(3):
                weight_out(p, k).wait()

        @pl.when(jnp.logical_not(away))
        def _():
            for k in range(3):
                weight_in(p, k).wait()

    for j in range(CHUNKS):
        for k in range(4):
            if j == 0 and k == 0:
                a2a(j, k).wait()
            else:
                a2a(j, k).wait_recv()
        own(j, 0).start()
        own(j, 1).start()
        share(j, 0, core).start()
        if j == 1:
            start_weights(0)

    for j in range(CHUNKS):
        own_in(j, 0).wait_recv()
        forward(j, 0).start()
        share(j, 3, core).start()
        own_in(j, 1).wait_recv()
        forward(j, 1).start()
        share(j, 1, core).start()
        if j == 1:
            start_weights(1)

    def half_rows(half):
        return pl.ds(pl.multiple_of(half * HALF, HALF), HALF)

    def terms(j, half, p):
        rs = half_rows(half)
        first, n = PIECES[p]
        both = jnp.dot(
            rows[j, 0, rs, :], gu_v[:, 2 * first : 2 * (first + n)], preferred_element_type=F32
        )
        gate, up = both[:, :n], both[:, n:]
        hidden = lax.dot_general(
            rows[j, 1, rs, :], down_v[first : first + n, :], NT, preferred_element_type=F32
        )
        sigma = jax.nn.sigmoid(gate)
        slope = sigma * (1.0 + gate * (1.0 - sigma))
        terms_v[j, rs, 2 * first : 2 * first + n] = (hidden * up * slope).astype(BF16)
        terms_v[j, rs, 2 * first + n : 2 * (first + n)] = (hidden * gate * sigma).astype(BF16)

    def products(j, half, ch, received):
        rs = half_rows(half)

        def columns(n, carry):
            cs = pl.ds(pl.multiple_of(ch * WIDE + n * COLS, COLS), COLS)
            part = lax.dot_general(terms_v[j, rs, :], gu_v[cs, :], NT, preferred_element_type=F32)
            if received:
                part += rows[j, 1, half_rows(other), cs].astype(F32)
            rows[j, 0, rs, cs] = part.astype(BF16)
            return carry

        lax.fori_loop(0, WIDE // COLS, columns, 0)

    def landing(first, n):
        return pl.ds(pl.multiple_of(core * HALF + first, BLOCK // 2), n)

    def add(j, at, n, ch, sources):
        def body(k, carry):
            cs = pl.ds(pl.multiple_of(ch * WIDE + k * COLS, COLS), COLS)
            total = rows[j, 0, at, cs].astype(F32)
            for first in sources:
                total += rows[j, 1, landing(first, n), cs].astype(F32)
            rows[j, 0, at, cs] = total.astype(BF16)
            return carry

        lax.fori_loop(0, WIDE // COLS, body, 0)

    def wide(ch):
        return pl.ds(ch * WIDE, WIDE)

    def sib(j, ch):
        src = rows.at[j, 0, half_rows(other), wide(ch)]
        dst = rows.at[j, 1, half_rows(core), wide(ch)]
        return remote(src, dst, sib_s.at[j, ch], sib_r.at[j, ch], sibling)

    def half_sum(j, ch, direction):
        first = direction * (BLOCK // 2)
        src = rows.at[j, 0, rds(core, y_far, first, BLOCK // 2), wide(ch)]
        dst = rows.at[j, 1, landing(first, BLOCK // 2), wide(ch)]
        k = 2 * ch + direction
        return remote(src, dst, half_s.at[j, k], half_r.at[j, k], (right, left)[direction])

    def full_sum(j, ch, direction):
        src = rows.at[j, 0, rds(core, (y_right, y_left)[direction]), wide(ch)]
        dst = rows.at[j, 1, landing(BLOCK * (1 + direction), BLOCK), wide(ch)]
        k = 2 * ch + direction
        return remote(src, dst, full_s.at[j, k], full_r.at[j, k], (right, left)[direction])

    def back_refs(j, ch, k):
        src = rows.at[j, 0, rds(core, y, k * SLOTS, SLOTS), wide(ch)]
        dst = ret.at[pl.ds(pl.multiple_of(mine * SLOTS, SLOTS), SLOTS), wide(ch)]
        return src, dst

    def back(j, ch, k):
        src, dst = back_refs(j, ch, k)
        dx, dz = step_of(j, k)
        who = place(mod4(x - dx), y, mod4(z - dz), core)
        return remote(src, dst, ret_s.at[j * 4 + k, ch], ret_r.at[j * 4 + k, ch], who)

    def local_back(ch):
        src, dst = back_refs(0, ch, 0)
        return pltpu.make_async_copy(src, dst, ret_r.at[0, ch])

    def stage_half(j, ch):
        half_sum(j, ch, 0).wait_recv()
        add(j, rds(core, y_right, 0, BLOCK // 2), BLOCK // 2, ch, [0])
        full_sum(j, ch, 0).start()
        half_sum(j, ch, 1).wait_recv()
        add(j, rds(core, y_left, BLOCK // 2, BLOCK // 2), BLOCK // 2, ch, [BLOCK // 2])
        full_sum(j, ch, 1).start()

    def stage_full(j, ch):
        full_sum(j, ch, 0).wait_recv()
        full_sum(j, ch, 1).wait_recv()
        add(j, rds(core, y), BLOCK, ch, [BLOCK, 2 * BLOCK])
        for k in range(1, 4):
            back(j, ch, k).start()

        if isinstance(j, int):
            (back(j, ch, 0) if j else local_back(ch)).start()
            return
        back(j, ch, 0).start()

    def early(j, carry):
        forward_in(j, 0).wait_recv()
        forward_in(j, 1).wait_recv()
        share(j, 2, core).start()
        for k in range(4):
            share(j, k, other).wait_recv()

        @pl.when(j == 0)
        def _():
            wait_weights(0)

        terms(j, other, 0)
        terms(j, core, 0)
        for direction in range(2):
            own(j, direction).wait_send()
            forward(j, direction).wait_send()
        for k in range(4):
            share(j, k, core).wait_send()
        return carry

    lax.fori_loop(0, CHUNKS, early, 0)
    wait_weights(1)

    def give(j, ch):
        products(j, other, ch, False)
        if ch == 0:
            pl.semaphore_wait(cr_sib, 1)
        sib(j, ch).start()

    def take(j, ch):
        sib(j, ch).wait_recv()
        products(j, core, ch, True)
        if ch == 0:
            pl.semaphore_wait(cr_right, 1)
            pl.semaphore_wait(cr_left, 1)
        half_sum(j, ch, 0).start()
        half_sum(j, ch, 1).start()

    def step(i, carry):
        j = CHUNKS - 1 - i

        def earlier(stage, ch):
            @pl.when(i >= 1)
            def _():
                stage(j + 1, ch)

        terms(j, other, 1)
        pl.semaphore_signal(cr_sib, inc=1, device_id=sibling, device_id_type=MESH)
        terms(j, core, 1)
        pl.semaphore_signal(cr_right, inc=1, device_id=left, device_id_type=MESH)
        pl.semaphore_signal(cr_left, inc=1, device_id=right, device_id_type=MESH)
        give(j, 0)
        earlier(stage_half, WIDTHS - 1)
        for ch in range(1, WIDTHS):
            give(j, ch)
            take(j, ch - 1)
            earlier(stage_full, ch - 1)
        take(j, WIDTHS - 1)
        earlier(stage_full, WIDTHS - 1)
        for ch in range(WIDTHS - 1):
            stage_half(j, ch)
        return carry

    lax.fori_loop(0, CHUNKS, step, 0)
    stage_half(0, WIDTHS - 1)
    for ch in range(WIDTHS):
        stage_full(0, ch)

    for ch in range(WIDTHS):
        local_back(ch).wait()
        for k in range(1, 16):
            back(k // 4, ch, k % 4).wait_recv()

        def pick(n, carry):
            cs = pl.ds(pl.multiple_of(ch * WIDE + n * COLS, COLS), COLS)
            out[:, cs] = jnp.dot(onehot_t[...], ret[:, cs], preferred_element_type=F32).astype(BF16)
            return carry

        lax.fori_loop(0, WIDE // COLS, pick, 0)

    for k in range(1, 16):
        a2a(k // 4, k % 4).wait_send()
        for ch in range(WIDTHS):
            back(k // 4, ch, k % 4).wait_send()

    def finish(j, carry):
        for ch in range(WIDTHS):
            sib(j, ch).wait_send()
            for direction in range(2):
                half_sum(j, ch, direction).wait_send()
                full_sum(j, ch, direction).wait_send()
        return carry

    lax.fori_loop(0, CHUNKS, finish, 0)


def shards(tokens, grad_out, route_prob, expert_index, w_gate, w_up, w_down):
    vmem = pl.BlockSpec(memory_space=pltpu.VMEM)
    hbm = pl.BlockSpec(memory_space=pl.ANY)
    dma = pltpu.SemaphoreType.DMA
    regular = pltpu.SemaphoreType.REGULAR
    n_tok = tokens.shape[0]
    return pl.pallas_call(
        kernel,
        out_shape=jax.ShapeDtypeStruct((n_tok, D), BF16),
        in_specs=[hbm] * 2 + [vmem] * 2 + [hbm] * 3,
        out_specs=vmem,
        scratch_shapes=[
            pltpu.VMEM((CHUNKS, 2, ROWS, D), BF16),
            pltpu.VMEM((D, 2 * UNITS), BF16),
            pltpu.VMEM((UNITS, D), BF16),
            pltpu.VMEM((2, HALF, D), BF16),
            pltpu.VMEM((EXPERTS * SLOTS, D), BF16),
            pltpu.VMEM((CHUNKS, ROWS, 2 * UNITS), BF16),
            pltpu.VMEM((n_tok, EXPERTS * SLOTS), BF16),
            pltpu.VMEM((n_tok, D), BF16),
            pltpu.VMEM((n_tok, D), BF16),
            dma((2,)),
            dma((16,)), dma((16,)),
            dma((CHUNKS, 2)), dma((CHUNKS, 2)),
            dma((CHUNKS, 2)), dma((CHUNKS, 2)),
            dma((CHUNKS, 4)), dma((CHUNKS, 4)),
            dma((2, 3)), dma((2, 3)),
            dma((CHUNKS, WIDTHS)), dma((CHUNKS, WIDTHS)),
            dma((CHUNKS, 2 * WIDTHS)), dma((CHUNKS, 2 * WIDTHS)),
            dma((CHUNKS, 2 * WIDTHS)), dma((CHUNKS, 2 * WIDTHS)),
            dma((16, WIDTHS)), dma((16, WIDTHS)),
            regular, regular, regular,
        ],
        compiler_params=pltpu.CompilerParams(
            collective_id=1, has_side_effects=True, vmem_limit_bytes=63 * 1024 * 1024
        ),
        cost_estimate=pl.CostEstimate(
            flops=2 * CHUNKS * ROWS * D * UNITS * 5, bytes_accessed=64 << 20, transcendentals=0
        ),
    )(
        tokens, grad_out, route_prob.reshape(1, n_tok), expert_index.reshape(1, n_tok),
        w_gate[0], w_up[0], w_down[0],
    )


def solution(mesh):
    return jax.shard_map(
        shards,
        mesh=mesh,
        in_specs=(
            P(("expert", "etp"), None),
            P(("expert", "etp"), None),
            P(("expert", "etp")),
            P(("expert", "etp"), None),
            P("expert", None, "etp"),
            P("expert", None, "etp"),
            P("expert", "etp", None),
        ),
        out_specs=P(("expert", "etp"), None),
        check_vma=False,
    )
```

```python
import functools

import jax
import jax.numpy as jnp
from jax import lax
from jax.experimental import pallas as pl
from jax.experimental.pallas import tpu as pltpu
from jax.sharding import PartitionSpec as P

MESH = pl.DeviceIdType.MESH
BF16 = jnp.bfloat16
F32 = jnp.float32
D = 4096
UNITS = 512
CHUNKS = 4
SLOTS = 16
BLOCK = 4 * SLOTS
HALF = 4 * BLOCK
ROWS = 2 * HALF
EXPERTS = 16
COLS = 512
PIECES = ((0, 384), (384, 128))
WIDTHS = 4
WIDE = D // WIDTHS
STEPS = (
    ((0, 0), (1, 1), (2, 2), (3, 3)),
    ((1, 0), (2, 1), (3, 2), (0, 3)),
    ((2, 0), (3, 1), (0, 2), (1, 3)),
    ((3, 0), (0, 1), (1, 2), (2, 3)),
)
NT = (((1,), (1,)), ((), ()))


def mod4(value):
    return lax.rem(value + 8, 4)


def step_of(j, k):
    if isinstance(j, int):
        return STEPS[j][k]
    dx, dz = STEPS[0][k]
    for t in range(1, CHUNKS):
        dx = jnp.where(j == t, STEPS[t][k][0], dx)
        dz = jnp.where(j == t, STEPS[t][k][1], dz)
    return dx, dz


def place(x, y, z, core):
    return (lax.rem(z, 2) * 4 + x) * 2 + core, y * 2 + z // 2


def kernel(
    tok_h, grad_h, prob, index, w_gate, w_up, w_down,
    out,
    rows, gu_v, down_v, send, ret, terms_v, onehot_t, tok, grad, in_s,
    a2a_s, a2a_r, ag_s, ag_r, fw_s, fw_r, sh_s, sh_r, w_s, w_r,
    sib_s, sib_r, half_s, half_r, full_s, full_r, ret_s, ret_r,
    cr_sib, cr_left, cr_right,
):
    e = lax.axis_index("expert")
    t = lax.axis_index("etp")
    core = lax.rem(e, 2)
    x = lax.rem(e // 2, 4)
    y = t // 2
    z_hi = lax.rem(t, 2)
    z = z_hi * 2 + e // 8
    other = 1 - core
    mine = (lax.rem(z, 2) * 4 + x) * 2 + z_hi
    y_right, y_left, y_far = mod4(y + 1), mod4(y - 1), mod4(y + 2)
    right, left = place(x, y_right, z, core), place(x, y_left, z, core)
    sibling = place(x, y, z, other)
    partner = place(x, y, mod4(z + 2), other)
    away = core != z_hi

    tok_in = pltpu.make_async_copy(tok_h, tok, in_s.at[0])
    grad_in = pltpu.make_async_copy(grad_h, grad, in_s.at[1])
    tok_in.start()
    grad_in.start()

    barrier = pltpu.get_barrier_semaphore()

    def greet(who):
        pl.semaphore_signal(barrier, inc=1, device_id=who, device_id_type=MESH)

    for k in range(1, 16):
        greet(place(mod4(x + k // 4), y, mod4(z + k % 4), core))
    for who in (right, left, sibling, partner):
        greet(who)

    n_tok = tok.shape[0]
    at_row = lax.broadcasted_iota(jnp.int32, (n_tok, n_tok), 0)
    at_col = lax.broadcasted_iota(jnp.int32, (n_tok, n_tok), 1)
    earlier = (at_row < at_col).astype(BF16)
    same = (at_row == at_col).astype(F32)
    ids = index[...]
    chosen = (lax.broadcasted_iota(jnp.int32, (EXPERTS, n_tok), 0) == ids).astype(F32)
    before = jnp.dot(chosen.astype(BF16), earlier, preferred_element_type=F32)
    slot = ids.astype(F32) * SLOTS + jnp.sum(before * chosen, axis=0, keepdims=True)
    slot_col = jnp.sum(same * slot, axis=1, keepdims=True)
    scale = jnp.sum(same * prob[...], axis=1, keepdims=True)
    n_slot = EXPERTS * SLOTS
    onehot = (lax.broadcasted_iota(jnp.int32, (n_slot, n_tok), 0).astype(F32) == slot).astype(BF16)
    onehot_t[...] = (
        lax.broadcasted_iota(jnp.int32, (n_tok, n_slot), 1).astype(F32) == slot_col
    ).astype(BF16)

    def fill(n, carry):
        cs = pl.ds(pl.multiple_of(n * COLS, COLS), COLS)
        send[0, :, cs] = jnp.dot(onehot, tok[:, cs], preferred_element_type=F32).astype(BF16)
        scaled = (scale * grad[:, cs].astype(F32)).astype(BF16)
        send[1, :, cs] = jnp.dot(onehot, scaled, preferred_element_type=F32).astype(BF16)
        return carry

    tok_in.wait()
    grad_in.wait()
    lax.fori_loop(0, D // COLS, fill, 0)
    pl.semaphore_wait(barrier, 19)

    def remote(src, dst, s, r, who):
        return pltpu.make_async_remote_copy(
            src_ref=src, dst_ref=dst, send_sem=s, recv_sem=r, device_id=who, device_id_type=MESH
        )

    def rds(half, yo, off=0, n=BLOCK):
        return pl.ds(pl.multiple_of(half * HALF + yo * BLOCK + off, SLOTS), n)

    def a2a(j, k):
        dx, dz = step_of(j, k)
        xd, zd = mod4(x + dx), mod4(z + dz)
        ed = (lax.rem(zd, 2) * 4 + xd) * 2 + zd // 2
        src = send.at[:, pl.ds(pl.multiple_of(ed * SLOTS, SLOTS), SLOTS), :]
        dst = rows.at[j, :, rds(core, y, k * SLOTS, SLOTS), :]
        if j == 0 and k == 0:
            return pltpu.make_async_copy(src, dst, a2a_r.at[0])
        return remote(src, dst, a2a_s.at[j * 4 + k], a2a_r.at[j * 4 + k], place(xd, y, zd, core))

    for j in range(CHUNKS):
        for k in range(4):
            a2a(j, k).start()

    def own(j, direction):
        ref = rows.at[j, :, rds(core, y), :]
        return remote(ref, ref, ag_s.at[j, direction], ag_r.at[j, direction], (right, left)[direction])

    def own_in(j, direction):
        ref = rows.at[j, :, rds(core, (y_left, y_right)[direction]), :]
        return remote(ref, ref, ag_s.at[j, direction], ag_r.at[j, direction], (right, left)[direction])

    def forward(j, direction):
        ref = rows.at[j, direction, rds(core, (y_left, y_right)[direction]), :]
        return remote(ref, ref, fw_s.at[j, direction], fw_r.at[j, direction], (right, left)[direction])

    def forward_in(j, direction):
        ref = rows.at[j, direction, rds(core, y_far), :]
        return remote(ref, ref, fw_s.at[j, direction], fw_r.at[j, direction], (right, left)[direction])

    def share(j, k, half):
        ref = rows.at[j, :, rds(half, mod4(y + k)), :]
        return remote(ref, ref, sh_s.at[j, k], sh_r.at[j, k], sibling)

    def weight_refs(p, k):
        first, n = PIECES[p]
        units = pl.ds(first, n)
        return (
            (w_gate.at[:, units], gu_v.at[:, pl.ds(2 * first, n)]),
            (w_up.at[:, units], gu_v.at[:, pl.ds(2 * first + n, n)]),
            (w_down.at[units, :], down_v.at[units, :]),
        )[k]

    def weight_in(p, k):
        src, dst = weight_refs(p, k)
        return pltpu.make_async_copy(src, dst, w_r.at[p, k])

    def weight_out(p, k):
        src, dst = weight_refs(p, k)
        return remote(src, dst, w_s.at[p, k], w_r.at[p, k], partner)

    def start_weights(p):
        @pl.when(away)
        def _():
            for k in range(3):
                weight_out(p, k).start()

        @pl.when(jnp.logical_not(away))
        def _():
            for k in range(3):
                weight_in(p, k).start()

    def wait_weights(p):
        @pl.when(away)
        def _():
            for k in range(3):
                weight_out(p, k).wait()

        @pl.when(jnp.logical_not(away))
        def _():
            for k in range(3):
                weight_in(p, k).wait()

    for j in range(CHUNKS):
        for k in range(4):
            if j == 0 and k == 0:
                a2a(j, k).wait()
            else:
                a2a(j, k).wait_recv()
        own(j, 0).start()
        own(j, 1).start()
        share(j, 0, core).start()
        if j == 1:
            start_weights(0)

    for j in range(CHUNKS):
        own_in(j, 0).wait_recv()
        forward(j, 0).start()
        share(j, 3, core).start()
        own_in(j, 1).wait_recv()
        forward(j, 1).start()
        share(j, 1, core).start()
        if j == 1:
            start_weights(1)

    def half_rows(half):
        return pl.ds(pl.multiple_of(half * HALF, HALF), HALF)

    def terms(j, half, p):
        rs = half_rows(half)
        first, n = PIECES[p]
        both = jnp.dot(
            rows[j, 0, rs, :], gu_v[:, 2 * first : 2 * (first + n)], preferred_element_type=F32
        )
        gate, up = both[:, :n], both[:, n:]
        hidden = lax.dot_general(
            rows[j, 1, rs, :], down_v[first : first + n, :], NT, preferred_element_type=F32
        )
        sigma = jax.nn.sigmoid(gate)
        slope = sigma * (1.0 + gate * (1.0 - sigma))
        terms_v[j, rs, 2 * first : 2 * first + n] = (hidden * up * slope).astype(BF16)
        terms_v[j, rs, 2 * first + n : 2 * (first + n)] = (hidden * gate * sigma).astype(BF16)

    def products(j, half, ch, received):
        rs = half_rows(half)

        def columns(n, carry):
            cs = pl.ds(pl.multiple_of(ch * WIDE + n * COLS, COLS), COLS)
            part = lax.dot_general(terms_v[j, rs, :], gu_v[cs, :], NT, preferred_element_type=F32)
            if received:
                part += rows[j, 1, half_rows(other), cs].astype(F32)
            rows[j, 0, rs, cs] = part.astype(BF16)
            return carry

        lax.fori_loop(0, WIDE // COLS, columns, 0, unroll=True)

    def landing(first, n):
        return pl.ds(pl.multiple_of(core * HALF + first, BLOCK // 2), n)

    def add(j, at, n, ch, sources):
        def body(k, carry):
            cs = pl.ds(pl.multiple_of(ch * WIDE + k * COLS, COLS), COLS)
            total = rows[j, 0, at, cs].astype(F32)
            for first in sources:
                total += rows[j, 1, landing(first, n), cs].astype(F32)
            rows[j, 0, at, cs] = total.astype(BF16)
            return carry

        lax.fori_loop(0, WIDE // COLS, body, 0, unroll=True)

    def wide(ch):
        return pl.ds(ch * WIDE, WIDE)

    def sib(j, ch):
        src = rows.at[j, 0, half_rows(other), wide(ch)]
        dst = rows.at[j, 1, half_rows(core), wide(ch)]
        return remote(src, dst, sib_s.at[j, ch], sib_r.at[j, ch], sibling)

    def half_sum(j, ch, direction):
        first = direction * (BLOCK // 2)
        src = rows.at[j, 0, rds(core, y_far, first, BLOCK // 2), wide(ch)]
        dst = rows.at[j, 1, landing(first, BLOCK // 2), wide(ch)]
        k = 2 * ch + direction
        return remote(src, dst, half_s.at[j, k], half_r.at[j, k], (right, left)[direction])

    def full_sum(j, ch, direction):
        src = rows.at[j, 0, rds(core, (y_right, y_left)[direction]), wide(ch)]
        dst = rows.at[j, 1, landing(BLOCK * (1 + direction), BLOCK), wide(ch)]
        k = 2 * ch + direction
        return remote(src, dst, full_s.at[j, k], full_r.at[j, k], (right, left)[direction])

    def back_refs(j, ch, k):
        src = rows.at[j, 0, rds(core, y, k * SLOTS, SLOTS), wide(ch)]
        dst = ret.at[pl.ds(pl.multiple_of(mine * SLOTS, SLOTS), SLOTS), wide(ch)]
        return src, dst

    def back(j, ch, k):
        src, dst = back_refs(j, ch, k)
        dx, dz = step_of(j, k)
        who = place(mod4(x - dx), y, mod4(z - dz), core)
        return remote(src, dst, ret_s.at[j * 4 + k, ch], ret_r.at[j * 4 + k, ch], who)

    def local_back(ch):
        src, dst = back_refs(0, ch, 0)
        return pltpu.make_async_copy(src, dst, ret_r.at[0, ch])

    def stage_half(j, ch):
        half_sum(j, ch, 0).wait_recv()
        add(j, rds(core, y_right, 0, BLOCK // 2), BLOCK // 2, ch, [0])
        full_sum(j, ch, 0).start()
        half_sum(j, ch, 1).wait_recv()
        add(j, rds(core, y_left, BLOCK // 2, BLOCK // 2), BLOCK // 2, ch, [BLOCK // 2])
        full_sum(j, ch, 1).start()

    def stage_full(j, ch):
        full_sum(j, ch, 0).wait_recv()
        full_sum(j, ch, 1).wait_recv()
        add(j, rds(core, y), BLOCK, ch, [BLOCK, 2 * BLOCK])
        for k in range(1, 4):
            back(j, ch, k).start()

        if isinstance(j, int):
            (back(j, ch, 0) if j else local_back(ch)).start()
            return
        back(j, ch, 0).start()

    def early(j, carry):
        forward_in(j, 0).wait_recv()
        forward_in(j, 1).wait_recv()
        share(j, 2, core).start()
        for k in range(4):
            share(j, k, other).wait_recv()

        @pl.when(j == 0)
        def _():
            wait_weights(0)

        terms(j, other, 0)
        terms(j, core, 0)
        for direction in range(2):
            own(j, direction).wait_send()
            forward(j, direction).wait_send()
        for k in range(4):
            share(j, k, core).wait_send()
        return carry

    lax.fori_loop(0, CHUNKS, early, 0)
    wait_weights(1)

    def give(j, ch):
        products(j, other, ch, False)
        if ch == 0:
            pl.semaphore_wait(cr_sib, 1)
        sib(j, ch).start()

    def take(j, ch):
        sib(j, ch).wait_recv()
        products(j, core, ch, True)
        if ch == 0:
            pl.semaphore_wait(cr_right, 1)
            pl.semaphore_wait(cr_left, 1)
        half_sum(j, ch, 0).start()
        half_sum(j, ch, 1).start()

    def step(i, carry):
        j = CHUNKS - 1 - i

        def earlier(stage, ch):
            @pl.when(i >= 1)
            def _():
                stage(j + 1, ch)

        terms(j, other, 1)
        pl.semaphore_signal(cr_sib, inc=1, device_id=sibling, device_id_type=MESH)
        terms(j, core, 1)
        pl.semaphore_signal(cr_right, inc=1, device_id=left, device_id_type=MESH)
        pl.semaphore_signal(cr_left, inc=1, device_id=right, device_id_type=MESH)
        give(j, 0)
        earlier(stage_half, WIDTHS - 1)
        for ch in range(1, WIDTHS):
            give(j, ch)
            take(j, ch - 1)
            earlier(stage_full, ch - 1)
        take(j, WIDTHS - 1)
        earlier(stage_full, WIDTHS - 1)
        for ch in range(WIDTHS - 1):
            stage_half(j, ch)
        return carry

    lax.fori_loop(0, CHUNKS, step, 0)
    stage_half(0, WIDTHS - 1)
    for ch in range(WIDTHS):
        stage_full(0, ch)

    for ch in range(WIDTHS):
        local_back(ch).wait()
        for k in range(1, 16):
            back(k // 4, ch, k % 4).wait_recv()

        def pick(n, carry):
            cs = pl.ds(pl.multiple_of(ch * WIDE + n * COLS, COLS), COLS)
            out[:, cs] = jnp.dot(onehot_t[...], ret[:, cs], preferred_element_type=F32).astype(BF16)
            return carry

        lax.fori_loop(0, WIDE // COLS, pick, 0)

    for k in range(1, 16):
        a2a(k // 4, k % 4).wait_send()
        for ch in range(WIDTHS):
            back(k // 4, ch, k % 4).wait_send()

    def finish(j, carry):
        for ch in range(WIDTHS):
            sib(j, ch).wait_send()
            for direction in range(2):
                half_sum(j, ch, direction).wait_send()
                full_sum(j, ch, direction).wait_send()
        return carry

    lax.fori_loop(0, CHUNKS, finish, 0)


def shards(tokens, grad_out, route_prob, expert_index, w_gate, w_up, w_down):
    vmem = pl.BlockSpec(memory_space=pltpu.VMEM)
    hbm = pl.BlockSpec(memory_space=pl.ANY)
    dma = pltpu.SemaphoreType.DMA
    regular = pltpu.SemaphoreType.REGULAR
    n_tok = tokens.shape[0]
    return pl.pallas_call(
        kernel,
        out_shape=jax.ShapeDtypeStruct((n_tok, D), BF16),
        in_specs=[hbm] * 2 + [vmem] * 2 + [hbm] * 3,
        out_specs=vmem,
        scratch_shapes=[
            pltpu.VMEM((CHUNKS, 2, ROWS, D), BF16),
            pltpu.VMEM((D, 2 * UNITS), BF16),
            pltpu.VMEM((UNITS, D), BF16),
            pltpu.VMEM((2, HALF, D), BF16),
            pltpu.VMEM((EXPERTS * SLOTS, D), BF16),
            pltpu.VMEM((CHUNKS, ROWS, 2 * UNITS), BF16),
            pltpu.VMEM((n_tok, EXPERTS * SLOTS), BF16),
            pltpu.VMEM((n_tok, D), BF16),
            pltpu.VMEM((n_tok, D), BF16),
            dma((2,)),
            dma((16,)), dma((16,)),
            dma((CHUNKS, 2)), dma((CHUNKS, 2)),
            dma((CHUNKS, 2)), dma((CHUNKS, 2)),
            dma((CHUNKS, 4)), dma((CHUNKS, 4)),
            dma((2, 3)), dma((2, 3)),
            dma((CHUNKS, WIDTHS)), dma((CHUNKS, WIDTHS)),
            dma((CHUNKS, 2 * WIDTHS)), dma((CHUNKS, 2 * WIDTHS)),
            dma((CHUNKS, 2 * WIDTHS)), dma((CHUNKS, 2 * WIDTHS)),
            dma((16, WIDTHS)), dma((16, WIDTHS)),
            regular, regular, regular,
        ],
        compiler_params=pltpu.CompilerParams(
            collective_id=1, has_side_effects=True, vmem_limit_bytes=63 * 1024 * 1024
        ),
        cost_estimate=pl.CostEstimate(
            flops=2 * CHUNKS * ROWS * D * UNITS * 5, bytes_accessed=64 << 20, transcendentals=0
        ),
    )(
        tokens, grad_out, route_prob.reshape(1, n_tok), expert_index.reshape(1, n_tok),
        w_gate[0], w_up[0], w_down[0],
    )


def solution(mesh):
    return jax.shard_map(
        shards,
        mesh=mesh,
        in_specs=(
            P(("expert", "etp"), None),
            P(("expert", "etp"), None),
            P(("expert", "etp")),
            P(("expert", "etp"), None),
            P("expert", None, "etp"),
            P("expert", None, "etp"),
            P("expert", "etp", None),
        ),
        out_specs=P(("expert", "etp"), None),
        check_vma=False,
    )
```

```python
import functools

import jax
import jax.numpy as jnp
from jax import lax
from jax.experimental import pallas as pl
from jax.experimental.pallas import tpu as pltpu
from jax.sharding import PartitionSpec as P

MESH = pl.DeviceIdType.MESH
BF16 = jnp.bfloat16
F32 = jnp.float32
D = 4096
UNITS = 512
CHUNKS = 4
SLOTS = 16
BLOCK = 4 * SLOTS
HALF = 4 * BLOCK
ROWS = 2 * HALF
EXPERTS = 16
COLS = 512
PIECES = ((0, 384), (384, 128))
WIDTHS = 4
WIDE = D // WIDTHS
STEPS = (
    ((0, 0), (1, 1), (2, 2), (3, 3)),
    ((1, 0), (2, 1), (3, 2), (0, 3)),
    ((2, 0), (3, 1), (0, 2), (1, 3)),
    ((3, 0), (0, 1), (1, 2), (2, 3)),
)
NT = (((1,), (1,)), ((), ()))


def mod4(value):
    return lax.rem(value + 8, 4)


def step_of(j, k):
    if isinstance(j, int):
        return STEPS[j][k]
    dx, dz = STEPS[0][k]
    for t in range(1, CHUNKS):
        dx = jnp.where(j == t, STEPS[t][k][0], dx)
        dz = jnp.where(j == t, STEPS[t][k][1], dz)
    return dx, dz


def place(x, y, z, core):
    return (lax.rem(z, 2) * 4 + x) * 2 + core, y * 2 + z // 2


def kernel(
    tok_h, grad_h, prob, index, w_gate, w_up, w_down,
    out,
    rows, gu_v, down_v, send, ret, terms_v, onehot_t, tok, grad, in_s, out_s,
    a2a_s, a2a_r, ag_s, ag_r, fw_s, fw_r, sh_s, sh_r, w_s, w_r,
    sib_s, sib_r, half_s, half_r, full_s, full_r, ret_s, ret_r,
    cr_sib, cr_left, cr_right,
):
    e = lax.axis_index("expert")
    t = lax.axis_index("etp")
    core = lax.rem(e, 2)
    x = lax.rem(e // 2, 4)
    y = t // 2
    z_hi = lax.rem(t, 2)
    z = z_hi * 2 + e // 8
    other = 1 - core
    mine = (lax.rem(z, 2) * 4 + x) * 2 + z_hi
    y_right, y_left, y_far = mod4(y + 1), mod4(y - 1), mod4(y + 2)
    right, left = place(x, y_right, z, core), place(x, y_left, z, core)
    sibling = place(x, y, z, other)
    partner = place(x, y, mod4(z + 2), other)
    away = core != z_hi

    tok_in = pltpu.make_async_copy(tok_h, tok, in_s.at[0])
    grad_in = pltpu.make_async_copy(grad_h, grad, in_s.at[1])
    tok_in.start()
    grad_in.start()

    barrier = pltpu.get_barrier_semaphore()

    def greet(who):
        pl.semaphore_signal(barrier, inc=1, device_id=who, device_id_type=MESH)

    for k in range(1, 16):
        greet(place(mod4(x + k // 4), y, mod4(z + k % 4), core))
    for who in (right, left, sibling, partner):
        greet(who)

    n_tok = tok.shape[0]
    at_row = lax.broadcasted_iota(jnp.int32, (n_tok, n_tok), 0)
    at_col = lax.broadcasted_iota(jnp.int32, (n_tok, n_tok), 1)
    earlier = (at_row < at_col).astype(BF16)
    same = (at_row == at_col).astype(F32)
    ids = index[...]
    chosen = (lax.broadcasted_iota(jnp.int32, (EXPERTS, n_tok), 0) == ids).astype(F32)
    before = jnp.dot(chosen.astype(BF16), earlier, preferred_element_type=F32)
    slot = ids.astype(F32) * SLOTS + jnp.sum(before * chosen, axis=0, keepdims=True)
    slot_col = jnp.sum(same * slot, axis=1, keepdims=True)
    scale = jnp.sum(same * prob[...], axis=1, keepdims=True)
    n_slot = EXPERTS * SLOTS
    onehot = (lax.broadcasted_iota(jnp.int32, (n_slot, n_tok), 0).astype(F32) == slot).astype(BF16)
    onehot_t[...] = (
        lax.broadcasted_iota(jnp.int32, (n_tok, n_slot), 1).astype(F32) == slot_col
    ).astype(BF16)

    def fill(n, carry):
        cs = pl.ds(pl.multiple_of(n * COLS, COLS), COLS)
        send[0, :, cs] = jnp.dot(onehot, tok[:, cs], preferred_element_type=F32).astype(BF16)
        scaled = (scale * grad[:, cs].astype(F32)).astype(BF16)
        send[1, :, cs] = jnp.dot(onehot, scaled, preferred_element_type=F32).astype(BF16)
        return carry

    tok_in.wait()
    grad_in.wait()
    lax.fori_loop(0, D // COLS, fill, 0)
    pl.semaphore_wait(barrier, 19)

    def remote(src, dst, s, r, who):
        return pltpu.make_async_remote_copy(
            src_ref=src, dst_ref=dst, send_sem=s, recv_sem=r, device_id=who, device_id_type=MESH
        )

    def rds(half, yo, off=0, n=BLOCK):
        return pl.ds(pl.multiple_of(half * HALF + yo * BLOCK + off, SLOTS), n)

    def a2a(j, k):
        dx, dz = step_of(j, k)
        xd, zd = mod4(x + dx), mod4(z + dz)
        ed = (lax.rem(zd, 2) * 4 + xd) * 2 + zd // 2
        src = send.at[:, pl.ds(pl.multiple_of(ed * SLOTS, SLOTS), SLOTS), :]
        dst = rows.at[j, :, rds(core, y, k * SLOTS, SLOTS), :]
        if j == 0 and k == 0:
            return pltpu.make_async_copy(src, dst, a2a_r.at[0])
        return remote(src, dst, a2a_s.at[j * 4 + k], a2a_r.at[j * 4 + k], place(xd, y, zd, core))

    for j in range(CHUNKS):
        for k in range(4):
            a2a(j, k).start()

    def own(j, direction):
        ref = rows.at[j, :, rds(core, y), :]
        return remote(ref, ref, ag_s.at[j, direction], ag_r.at[j, direction], (right, left)[direction])

    def own_in(j, direction):
        ref = rows.at[j, :, rds(core, (y_left, y_right)[direction]), :]
        return remote(ref, ref, ag_s.at[j, direction], ag_r.at[j, direction], (right, left)[direction])

    def forward(j, direction):
        ref = rows.at[j, direction, rds(core, (y_left, y_right)[direction]), :]
        return remote(ref, ref, fw_s.at[j, direction], fw_r.at[j, direction], (right, left)[direction])

    def forward_in(j, direction):
        ref = rows.at[j, direction, rds(core, y_far), :]
        return remote(ref, ref, fw_s.at[j, direction], fw_r.at[j, direction], (right, left)[direction])

    def share(j, k, half):
        ref = rows.at[j, :, rds(half, mod4(y + k)), :]
        return remote(ref, ref, sh_s.at[j, k], sh_r.at[j, k], sibling)

    def weight_refs(p, k):
        first, n = PIECES[p]
        units = pl.ds(first, n)
        return (
            (w_gate.at[:, units], gu_v.at[:, pl.ds(2 * first, n)]),
            (w_up.at[:, units], gu_v.at[:, pl.ds(2 * first + n, n)]),
            (w_down.at[units, :], down_v.at[units, :]),
        )[k]

    def weight_in(p, k):
        src, dst = weight_refs(p, k)
        return pltpu.make_async_copy(src, dst, w_r.at[p, k])

    def weight_out(p, k):
        src, dst = weight_refs(p, k)
        return remote(src, dst, w_s.at[p, k], w_r.at[p, k], partner)

    def start_weights(p):
        @pl.when(away)
        def _():
            for k in range(3):
                weight_out(p, k).start()

        @pl.when(jnp.logical_not(away))
        def _():
            for k in range(3):
                weight_in(p, k).start()

    def wait_weights(p):
        @pl.when(away)
        def _():
            for k in range(3):
                weight_out(p, k).wait()

        @pl.when(jnp.logical_not(away))
        def _():
            for k in range(3):
                weight_in(p, k).wait()

    for j in range(CHUNKS):
        for k in range(4):
            if j == 0 and k == 0:
                a2a(j, k).wait()
            else:
                a2a(j, k).wait_recv()
        own(j, 0).start()
        own(j, 1).start()
        share(j, 0, core).start()
        if j == 1:
            start_weights(0)

    for j in range(CHUNKS):
        own_in(j, 0).wait_recv()
        forward(j, 0).start()
        share(j, 3, core).start()
        own_in(j, 1).wait_recv()
        forward(j, 1).start()
        share(j, 1, core).start()
        if j == 1:
            start_weights(1)

    def half_rows(half):
        return pl.ds(pl.multiple_of(half * HALF, HALF), HALF)

    def terms(j, half, p):
        rs = half_rows(half)
        first, n = PIECES[p]
        both = jnp.dot(
            rows[j, 0, rs, :], gu_v[:, 2 * first : 2 * (first + n)], preferred_element_type=F32
        )
        gate, up = both[:, :n], both[:, n:]
        hidden = lax.dot_general(
            rows[j, 1, rs, :], down_v[first : first + n, :], NT, preferred_element_type=F32
        )
        sigma = jax.nn.sigmoid(gate)
        slope = sigma * (1.0 + gate * (1.0 - sigma))
        terms_v[j, rs, 2 * first : 2 * first + n] = (hidden * up * slope).astype(BF16)
        terms_v[j, rs, 2 * first + n : 2 * (first + n)] = (hidden * gate * sigma).astype(BF16)

    def products(j, half, ch, received):
        rs = half_rows(half)

        def columns(n, carry):
            cs = pl.ds(pl.multiple_of(ch * WIDE + n * COLS, COLS), COLS)
            part = lax.dot_general(terms_v[j, rs, :], gu_v[cs, :], NT, preferred_element_type=F32)
            if received:
                part += rows[j, 1, half_rows(other), cs].astype(F32)
            rows[j, 0, rs, cs] = part.astype(BF16)
            return carry

        lax.fori_loop(0, WIDE // COLS, columns, 0, unroll=True)

    def landing(first, n):
        return pl.ds(pl.multiple_of(core * HALF + first, BLOCK // 2), n)

    def add(j, at, n, ch, sources):
        def body(k, carry):
            cs = pl.ds(pl.multiple_of(ch * WIDE + k * COLS, COLS), COLS)
            total = rows[j, 0, at, cs].astype(F32)
            for first in sources:
                total += rows[j, 1, landing(first, n), cs].astype(F32)
            rows[j, 0, at, cs] = total.astype(BF16)
            return carry

        lax.fori_loop(0, WIDE // COLS, body, 0, unroll=True)

    def wide(ch):
        return pl.ds(ch * WIDE, WIDE)

    def sib(j, ch):
        src = rows.at[j, 0, half_rows(other), wide(ch)]
        dst = rows.at[j, 1, half_rows(core), wide(ch)]
        return remote(src, dst, sib_s.at[j, ch], sib_r.at[j, ch], sibling)

    def half_sum(j, ch, direction):
        first = direction * (BLOCK // 2)
        src = rows.at[j, 0, rds(core, y_far, first, BLOCK // 2), wide(ch)]
        dst = rows.at[j, 1, landing(first, BLOCK // 2), wide(ch)]
        k = 2 * ch + direction
        return remote(src, dst, half_s.at[j, k], half_r.at[j, k], (right, left)[direction])

    def full_sum(j, ch, direction):
        src = rows.at[j, 0, rds(core, (y_right, y_left)[direction]), wide(ch)]
        dst = rows.at[j, 1, landing(BLOCK * (1 + direction), BLOCK), wide(ch)]
        k = 2 * ch + direction
        return remote(src, dst, full_s.at[j, k], full_r.at[j, k], (right, left)[direction])

    def back_refs(j, ch, k):
        src = rows.at[j, 0, rds(core, y, k * SLOTS, SLOTS), wide(ch)]
        dst = ret.at[pl.ds(pl.multiple_of(mine * SLOTS, SLOTS), SLOTS), wide(ch)]
        return src, dst

    def back(j, ch, k):
        src, dst = back_refs(j, ch, k)
        dx, dz = step_of(j, k)
        who = place(mod4(x - dx), y, mod4(z - dz), core)
        return remote(src, dst, ret_s.at[j * 4 + k, ch], ret_r.at[j * 4 + k, ch], who)

    def local_back(ch):
        src, dst = back_refs(0, ch, 0)
        return pltpu.make_async_copy(src, dst, ret_r.at[0, ch])

    def stage_half(j, ch):
        half_sum(j, ch, 0).wait_recv()
        add(j, rds(core, y_right, 0, BLOCK // 2), BLOCK // 2, ch, [0])
        full_sum(j, ch, 0).start()
        half_sum(j, ch, 1).wait_recv()
        add(j, rds(core, y_left, BLOCK // 2, BLOCK // 2), BLOCK // 2, ch, [BLOCK // 2])
        full_sum(j, ch, 1).start()

    def stage_full(j, ch):
        full_sum(j, ch, 0).wait_recv()
        full_sum(j, ch, 1).wait_recv()
        add(j, rds(core, y), BLOCK, ch, [BLOCK, 2 * BLOCK])
        for k in range(1, 4):
            back(j, ch, k).start()

        if isinstance(j, int):
            (back(j, ch, 0) if j else local_back(ch)).start()
            return
        back(j, ch, 0).start()

    def early(j, carry):
        forward_in(j, 0).wait_recv()
        forward_in(j, 1).wait_recv()
        share(j, 2, core).start()
        for k in range(4):
            share(j, k, other).wait_recv()

        @pl.when(j == 0)
        def _():
            wait_weights(0)

        terms(j, other, 0)
        terms(j, core, 0)
        for direction in range(2):
            own(j, direction).wait_send()
            forward(j, direction).wait_send()
        for k in range(4):
            share(j, k, core).wait_send()
        return carry

    lax.fori_loop(0, CHUNKS, early, 0)
    wait_weights(1)

    def give(j, ch):
        products(j, other, ch, False)
        if ch == 0:
            pl.semaphore_wait(cr_sib, 1)
        sib(j, ch).start()

    def take(j, ch):
        sib(j, ch).wait_recv()
        products(j, core, ch, True)
        if ch == 0:
            pl.semaphore_wait(cr_right, 1)
            pl.semaphore_wait(cr_left, 1)
        half_sum(j, ch, 0).start()
        half_sum(j, ch, 1).start()

    def step(i, carry):
        j = CHUNKS - 1 - i

        def earlier(stage, ch):
            @pl.when(i >= 1)
            def _():
                stage(j + 1, ch)

        terms(j, other, 1)
        pl.semaphore_signal(cr_sib, inc=1, device_id=sibling, device_id_type=MESH)
        terms(j, core, 1)
        pl.semaphore_signal(cr_right, inc=1, device_id=left, device_id_type=MESH)
        pl.semaphore_signal(cr_left, inc=1, device_id=right, device_id_type=MESH)
        give(j, 0)
        earlier(stage_half, WIDTHS - 1)
        for ch in range(1, WIDTHS):
            give(j, ch)
            take(j, ch - 1)
            earlier(stage_full, ch - 1)
        take(j, WIDTHS - 1)
        earlier(stage_full, WIDTHS - 1)
        @pl.when(j > 0)
        def _():
            for ch in range(WIDTHS - 1):
                stage_half(j, ch)

        return carry

    lax.fori_loop(0, CHUNKS, step, 0)
    for ch in range(WIDTHS + 2):
        if ch < WIDTHS:
            stage_half(0, ch)
        if ch >= 2:
            stage_full(0, ch - 2)

    def result(ch):
        return pltpu.make_async_copy(tok.at[:, wide(ch)], out.at[:, wide(ch)], out_s.at[ch])

    for ch in range(WIDTHS):
        local_back(ch).wait()
        for k in range(1, 16):
            back(k // 4, ch, k % 4).wait_recv()

        def pick(n, carry):
            cs = pl.ds(pl.multiple_of(ch * WIDE + n * COLS, COLS), COLS)
            tok[:, cs] = jnp.dot(onehot_t[...], ret[:, cs], preferred_element_type=F32).astype(BF16)
            return carry

        lax.fori_loop(0, WIDE // COLS, pick, 0, unroll=True)
        result(ch).start()

    for k in range(1, 16):
        a2a(k // 4, k % 4).wait_send()
        for ch in range(WIDTHS):
            back(k // 4, ch, k % 4).wait_send()

    def finish(j, carry):
        for ch in range(WIDTHS):
            sib(j, ch).wait_send()
            for direction in range(2):
                half_sum(j, ch, direction).wait_send()
                full_sum(j, ch, direction).wait_send()
        return carry

    lax.fori_loop(0, CHUNKS, finish, 0)
    for ch in range(WIDTHS):
        result(ch).wait()


def shards(tokens, grad_out, route_prob, expert_index, w_gate, w_up, w_down):
    vmem = pl.BlockSpec(memory_space=pltpu.VMEM)
    hbm = pl.BlockSpec(memory_space=pl.ANY)
    dma = pltpu.SemaphoreType.DMA
    regular = pltpu.SemaphoreType.REGULAR
    n_tok = tokens.shape[0]
    return pl.pallas_call(
        kernel,
        out_shape=jax.ShapeDtypeStruct((n_tok, D), BF16),
        in_specs=[hbm] * 2 + [vmem] * 2 + [hbm] * 3,
        out_specs=hbm,
        scratch_shapes=[
            pltpu.VMEM((CHUNKS, 2, ROWS, D), BF16),
            pltpu.VMEM((D, 2 * UNITS), BF16),
            pltpu.VMEM((UNITS, D), BF16),
            pltpu.VMEM((2, HALF, D), BF16),
            pltpu.VMEM((EXPERTS * SLOTS, D), BF16),
            pltpu.VMEM((CHUNKS, ROWS, 2 * UNITS), BF16),
            pltpu.VMEM((n_tok, EXPERTS * SLOTS), BF16),
            pltpu.VMEM((n_tok, D), BF16),
            pltpu.VMEM((n_tok, D), BF16),
            dma((2,)), dma((WIDTHS,)),
            dma((16,)), dma((16,)),
            dma((CHUNKS, 2)), dma((CHUNKS, 2)),
            dma((CHUNKS, 2)), dma((CHUNKS, 2)),
            dma((CHUNKS, 4)), dma((CHUNKS, 4)),
            dma((2, 3)), dma((2, 3)),
            dma((CHUNKS, WIDTHS)), dma((CHUNKS, WIDTHS)),
            dma((CHUNKS, 2 * WIDTHS)), dma((CHUNKS, 2 * WIDTHS)),
            dma((CHUNKS, 2 * WIDTHS)), dma((CHUNKS, 2 * WIDTHS)),
            dma((16, WIDTHS)), dma((16, WIDTHS)),
            regular, regular, regular,
        ],
        compiler_params=pltpu.CompilerParams(
            collective_id=1, has_side_effects=True, vmem_limit_bytes=63 * 1024 * 1024
        ),
        cost_estimate=pl.CostEstimate(
            flops=2 * CHUNKS * ROWS * D * UNITS * 5, bytes_accessed=64 << 20, transcendentals=0
        ),
    )(
        tokens, grad_out, route_prob.reshape(1, n_tok), expert_index.reshape(1, n_tok),
        w_gate[0], w_up[0], w_down[0],
    )


def solution(mesh):
    return jax.shard_map(
        shards,
        mesh=mesh,
        in_specs=(
            P(("expert", "etp"), None),
            P(("expert", "etp"), None),
            P(("expert", "etp")),
            P(("expert", "etp"), None),
            P("expert", None, "etp"),
            P("expert", None, "etp"),
            P("expert", "etp", None),
        ),
        out_specs=P(("expert", "etp"), None),
        check_vma=False,
    )
```
